128 devices in a mesh: dp: 8 (over x, core), expert: 16 (over y, z).
Axes of the slice: x: 4, y: 4, z: 4, core: 2. Of those that a mesh axis runs over, the one named last changes fastest.
Arguments:
- tokens: bfloat16 [32768, 4096], P(('dp', 'expert')), may hold values from -6 to 6
- cotangent: bfloat16 [32768, 4096], P(('dp', 'expert')), may hold values from -6 to 6
- routed_expert_index: int32 [32768, 2], P(('dp', 'expert')), may hold values from 0 to 15, all different within a row; in each aligned block of 256 rows (0 to 255, 256 to 511, ...) at most 40 rows name the same one
- router_gate_weights: float32 [32768, 2], P(('dp', 'expert')), may hold values from 0.05 to 1
- token_tenant_index: int32 [32768], P(('dp', 'expert')), may hold values from 0 to 7
- frozen_gate_weight: bfloat16 [16, 4096, 768], P('expert'), may hold values from -0.09375 to 0.09375
- frozen_up_weight: bfloat16 [16, 4096, 768], P('expert'), may hold values from -0.09375 to 0.09375
- frozen_down_weight: bfloat16 [16, 768, 4096], P('expert'), may hold values from -0.21875 to 0.21875
- adapter_down_matrices: bfloat16 [8, 16, 2, 16, 4096], P('dp', 'expert'), may hold values from -0.09375 to 0.09375
- adapter_up_matrices: bfloat16 [8, 16, 2, 16, 768], P('dp', 'expert'), may hold values from -1.5 to 1.5
Outputs:
- token_grads: bfloat16 [32768, 4096], P(('dp', 'expert'))
- down_grads: float32 [8, 16, 2, 16, 4096], P('dp', 'expert')
- up_grads: float32 [8, 16, 2, 16, 768], P('dp', 'expert')
The draws below stay inside these ranges and needn't reach their ends.
Inputs may be any that keep to these rules, and one draw needn't show every extreme that they name: `routed_expert_index`: a token's 2 experts differ; at most 40 routes of the tokens of one device go to one expert, and some device sends exactly 40 to some expert.
All inputs are finite; a program needn't handle non-finite values.
Results may differ from the reference program's by a relative error of at most 0.0068.
Values may be sent and summed in bfloat16 or wider, within the bound.
No kernel may reach another device: no remote copies, remote signals or barrier semaphores. Data moves between devices by JAX's collectives and lax.ppermute only.
A program may use at most 192 MiB of HBM per device.

```python
import math
import jax
import jax.numpy as jnp
import numpy as np
from jax import lax

MODEL_WIDTH = 4096
HIDDEN_HALF = 768
ADAPTER_RANK = 16
TENANT_TOTAL = 8
ROUTES = 2
TOK_DEV = 256
WINDOW_EXPERTS = 16
CAP = 40
TOKENS = 32768
N_DP = 8
N_EXPERT = 16


def place_ends(array, rng, least, largest):
    extent = array.shape
    index_at = [jax.random.randint(jax.random.fold_in(rng, axis), (), 0, extent[axis]) for axis in range(len(extent))]
    array = array.at[tuple(index_at)].set(least)
    longest = extent.index(max(extent))
    index_at[longest] = (index_at[longest] + 1) % extent[longest]
    return array.at[tuple(index_at)].set(largest)


def block_levels(key, dims, shards, least, high):
    def one(position, shards_of):
        heights = jax.random.uniform(jax.random.fold_in(jax.random.fold_in(key, 6), position), (shards_of,), jnp.float32, least / len(shards), high / len(shards))
        return jnp.repeat(jnp.exp(heights), dims[position] // shards_of).reshape((-1,) + (1,) * (len(dims) - position - 1))

    level = one(*shards[0])
    for cut in shards[1:]:
        level = level * one(*cut)
    return level


def assign_block(key, own, number, rows, count, top, most, slope):
    ranking = jax.random.permutation(key, count)
    heavy_load, usual = portions_of(count, rows * top, most, slope, True), portions_of(count, rows * top, most, slope, False)
    places = jnp.arange(count)

    def named(sizes, turn):
        used = int((sizes > 0).sum())
        fixed = max(1, used // 4)
        moved = fixed + (places - fixed + turn * (used - fixed)) % max(1, count - fixed)
        return jnp.zeros((count,), jnp.int32).at[ranking[jnp.where(places < fixed, places, moved)]].set(jnp.asarray(sizes, jnp.int32))

    sizes = jnp.where(number % 4 == 0, named(heavy_load, number // 4), named(usual, number - number // 4 - 1))
    mixed = jax.random.permutation(jax.random.fold_in(own, 3), count)
    giver, taker = mixed[0:count // 2 * 2:2], mixed[1:count // 2 * 2:2]
    slack = jnp.minimum(sizes[giver] - 1, most - sizes[taker]) // 2
    slack = jnp.where((giver == ranking[0]) | (taker == ranking[0]) | (sizes[taker] == 0), 0, jnp.maximum(slack, 0))
    moved = jax.random.randint(jax.random.fold_in(own, 4), (count // 2,), 0, 1 << 20) % (slack + 1)
    sizes = sizes.at[giver].add(-moved).at[taker].add(moved)
    members = jnp.searchsorted(jnp.cumsum(sizes), jnp.arange(rows * top), side="right").astype(jnp.int32)
    listing = members.reshape(top, rows).T
    listing = listing[jax.random.permutation(jax.random.fold_in(own, 1), rows)]
    turn = jax.random.randint(jax.random.fold_in(own, 2), (rows, 1), 0, top)
    return jnp.take_along_axis(listing, (jnp.arange(top)[None, :] + turn) % top, axis=1)


def portions_of(amount, total, most, lean, full):
    weights = [(1 << 20) // math.isqrt(grade ** lean) + 1 for grade in range(1, amount + 1)]
    largest = most if full else min(most, max(-(-total // amount), total * weights[0] // sum(weights)))
    least = 1 if total - largest >= amount - 1 else 0
    given, rest = [largest] + [least] * (amount - 1), total - largest - least * (amount - 1)
    while rest > 0:
        candidates = [i for i in range(1, amount) if given[i] < largest] or [i for i in range(1, amount) if given[i] < most]
        whole, left = sum([weights[i] for i in candidates]), rest
        for i in candidates:
            addition = min(most - given[i], max(1, left * weights[i] // whole), rest)
            given[i] = given[i] + addition
            rest = rest - addition
    return np.array(given)


def normal_values(stream_key, dims, spread, most, pieces=(), held_as=jnp.bfloat16):
    values = spread * jax.random.normal(stream_key, dims, jnp.float32)
    if pieces:
        values = values * block_levels(stream_key, dims, pieces, -0.22, 0.18)
    return jnp.clip(values, -most, most).astype(held_as)


def setup_inputs(seed: int = 0) -> dict:
    arg_keys = jax.random.split(jax.random.key(seed), 11)
    tokens = normal_values(arg_keys[0], (TOKENS, MODEL_WIDTH), 1.0, 6.0, ((0, 128),))
    cotangent = normal_values(arg_keys[1], (TOKENS, MODEL_WIDTH), 1.0, 6.0, ((0, 128),))
    routed_expert_index_keys = jax.random.split(jax.random.fold_in(arg_keys[2], 1), TOKENS // TOK_DEV)
    routed_expert_index_turns = jax.random.permutation(jax.random.fold_in(arg_keys[2], 3), TOKENS // TOK_DEV)
    routed_expert_index = jax.vmap(lambda own, number: assign_block(jax.random.fold_in(arg_keys[2], 2), own, number, TOK_DEV, WINDOW_EXPERTS, ROUTES, CAP, 1))(routed_expert_index_keys, routed_expert_index_turns).reshape((TOKENS, ROUTES))
    router_gate_weights = jnp.clip(jnp.exp(math.log(1.0) - 2.9957323 * jax.random.uniform(arg_keys[3], (TOKENS, ROUTES), jnp.float32) ** block_levels(arg_keys[3], (TOKENS, ROUTES), ((0, 128),), -0.2, 0.2)), 0.05, 1.0)
    token_tenant_index = place_ends(jax.random.randint(arg_keys[4], (TOKENS,), 0, TENANT_TOTAL), jax.random.fold_in(arg_keys[4], 1), 0, TENANT_TOTAL - 1).astype(jnp.int32)
    frozen_gate_weight = normal_values(arg_keys[5], (WINDOW_EXPERTS, MODEL_WIDTH, HIDDEN_HALF), MODEL_WIDTH ** -0.5, 0.09375, ((0, 16),))
    frozen_up_weight = normal_values(arg_keys[6], (WINDOW_EXPERTS, MODEL_WIDTH, HIDDEN_HALF), MODEL_WIDTH ** -0.5, 0.09375, ((0, 16),))
    frozen_down_weight = normal_values(arg_keys[7], (WINDOW_EXPERTS, HIDDEN_HALF, MODEL_WIDTH), HIDDEN_HALF ** -0.5, 0.21875, ((0, 16),))
    adapter_down_matrices = normal_values(arg_keys[8], (TENANT_TOTAL, WINDOW_EXPERTS, 2, ADAPTER_RANK, MODEL_WIDTH), MODEL_WIDTH ** -0.5, 0.09375, ((0, 8), (1, 16)))
    adapter_up_matrices = normal_values(arg_keys[9], (TENANT_TOTAL, WINDOW_EXPERTS, 2, ADAPTER_RANK, HIDDEN_HALF), ADAPTER_RANK ** -0.5, 1.5, ((0, 8), (1, 16)))
    return {"tokens": tokens, "cotangent": cotangent, "routed_expert_index": routed_expert_index, "router_gate_weights": router_gate_weights, "token_tenant_index": token_tenant_index, "frozen_gate_weight": frozen_gate_weight, "frozen_up_weight": frozen_up_weight, "frozen_down_weight": frozen_down_weight, "adapter_down_matrices": adapter_down_matrices, "adapter_up_matrices": adapter_up_matrices}


adapter_scale = 0.5


def contract_last(left_side, right_side):
    return lax.dot_general(left_side, right_side, (((1,), (1,)), ((), ())), preferred_element_type=jnp.float32)


def contract_first(left_side, right_side):
    return lax.dot_general(left_side, right_side, (((0,), (0,)), ((), ())), preferred_element_type=jnp.float32)


def tenant_mask(tenant_rows, tenant_count):
    return (tenant_rows[:, None] == jnp.arange(tenant_count, dtype=jnp.int32)[None, :]).astype(jnp.float32)


def forward_pass(input_features, tenant_rows, gate_matrix, up_matrix, down_adapter_groups, up_adapter_groups):
    tenant_count, _, rank_size, feature_width = down_adapter_groups.shape
    selector = tenant_mask(tenant_rows, tenant_count)
    low_all = contract_last(input_features, down_adapter_groups.reshape(tenant_count * 2 * rank_size, feature_width))
    low_all = (low_all.reshape(-1, tenant_count, 2, rank_size) * selector[:, :, None, None]).astype(jnp.bfloat16)
    gate_low = low_all[:, :, 0, :].reshape(-1, tenant_count * rank_size)
    up_low = low_all[:, :, 1, :].reshape(-1, tenant_count * rank_size)
    gate_preactivation = jnp.dot(input_features, gate_matrix, preferred_element_type=jnp.float32) + adapter_scale * jnp.dot(
        gate_low, up_adapter_groups[:, 0].reshape(tenant_count * rank_size, -1), preferred_element_type=jnp.float32)
    up_preactivation = jnp.dot(input_features, up_matrix, preferred_element_type=jnp.float32) + adapter_scale * jnp.dot(
        up_low, up_adapter_groups[:, 1].reshape(tenant_count * rank_size, -1), preferred_element_type=jnp.float32)
    return selector, gate_low, up_low, gate_preactivation, up_preactivation


def backward_pass(input_features, routed, saved_state, gate_matrix, up_matrix, down_weight, down_adapter_groups, up_adapter_groups):
    selector, gate_low, up_low, gate_preactivation, up_preactivation = saved_state
    tenant_count, _, rank_size, feature_width = down_adapter_groups.shape
    cot_back = contract_last(routed, down_weight)
    sigmoid_gate = jax.nn.sigmoid(gate_preactivation)
    gate_grad = (cot_back * up_preactivation * (sigmoid_gate + gate_preactivation * sigmoid_gate * (1.0 - sigmoid_gate))).astype(jnp.bfloat16)
    up_grad = (cot_back * gate_preactivation * sigmoid_gate).astype(jnp.bfloat16)

    def masked(values):
        shaped = values.reshape(-1, tenant_count, rank_size) * selector[:, :, None]
        return shaped.reshape(-1, tenant_count * rank_size).astype(jnp.bfloat16)

    gate_back = masked(contract_last(gate_grad, up_adapter_groups[:, 0].reshape(tenant_count * rank_size, -1)))
    up_back = masked(contract_last(up_grad, up_adapter_groups[:, 1].reshape(tenant_count * rank_size, -1)))
    gradient_total = contract_last(gate_grad, gate_matrix) + contract_last(up_grad, up_matrix)
    gradient_total = gradient_total + adapter_scale * (
        jnp.dot(gate_back, down_adapter_groups[:, 0].reshape(tenant_count * rank_size, feature_width), preferred_element_type=jnp.float32)
        + jnp.dot(up_back, down_adapter_groups[:, 1].reshape(tenant_count * rank_size, feature_width), preferred_element_type=jnp.float32))
    route_grad = gradient_total.astype(jnp.bfloat16)
    down_portion = adapter_scale * jnp.stack([
        contract_first(gate_back, input_features).reshape(tenant_count, rank_size, feature_width),
        contract_first(up_back, input_features).reshape(tenant_count, rank_size, feature_width)], axis=1)
    up_portion = adapter_scale * jnp.stack([
        contract_first(gate_low, gate_grad).reshape(tenant_count, rank_size, -1),
        contract_first(up_low, up_grad).reshape(tenant_count, rank_size, -1)], axis=1)
    return route_grad, down_portion, up_portion


def reference(tokens, cotangent, routed_expert_index, router_gate_weights, token_tenant_index, frozen_gate_weight, frozen_up_weight, frozen_down_weight, adapter_down_matrices, adapter_up_matrices):
    route_total = TOKENS * ROUTES
    limit = N_DP * N_EXPERT * CAP
    flat_expert = routed_expert_index.reshape(-1)
    flat_probs = router_gate_weights.reshape(-1)

    def per_expert(collected, expert_number):
        matches = flat_expert == expert_number
        row_index = jnp.nonzero(matches, size=limit, fill_value=0)[0].astype(jnp.int32)
        in_range = jnp.arange(limit, dtype=jnp.int32) < jnp.sum(matches.astype(jnp.int32))
        token_index = row_index // ROUTES
        input_features = jnp.where(in_range[:, None], tokens[token_index], jnp.zeros((), jnp.bfloat16)).astype(jnp.bfloat16)
        weights = jnp.where(in_range, flat_probs[row_index], 0.0).astype(jnp.float32)
        routed = (weights[:, None] * cotangent[token_index].astype(jnp.float32)).astype(jnp.bfloat16)
        tenant_rows = token_tenant_index[token_index]
        down_adapter_groups = adapter_down_matrices[:, expert_number]
        up_adapter_groups = adapter_up_matrices[:, expert_number]
        saved_state = forward_pass(input_features, tenant_rows, frozen_gate_weight[expert_number], frozen_up_weight[expert_number], down_adapter_groups, up_adapter_groups)
        route_grad, down_portion, up_portion = backward_pass(input_features, routed, saved_state, frozen_gate_weight[expert_number], frozen_up_weight[expert_number],
                                                       frozen_down_weight[expert_number], down_adapter_groups, up_adapter_groups)
        target = jnp.where(in_range, row_index, route_total).astype(jnp.int32)
        collected = collected.at[target].set(route_grad, mode="drop")
        return collected, (down_portion, up_portion)

    start = jnp.zeros((route_total, MODEL_WIDTH), jnp.bfloat16)
    collected, (down_all, up_all) = lax.scan(per_expert, start, jnp.arange(WINDOW_EXPERTS, dtype=jnp.int32))
    token_grads = jnp.sum(collected.reshape(TOKENS, ROUTES, MODEL_WIDTH).astype(jnp.float32), axis=1).astype(jnp.bfloat16)
    down_grads = jnp.transpose(down_all, (1, 0, 2, 3, 4))
    up_grads = jnp.transpose(up_all, (1, 0, 2, 3, 4))
    return (token_grads, down_grads, up_grads)
```

```python
import functools

import jax
import jax.numpy as jnp
from jax import lax
from jax.experimental import pallas as pl
from jax.experimental.pallas import tpu as pltpu
from jax.sharding import PartitionSpec as P

adapter_scale = 0.5
LANES = 128
CHUNKS = ((0, 24), (24, 40))
VMEM_BYTES = 56 * 1024 * 1024


def contract_last(left_side, right_side):
    return lax.dot_general(
        left_side, right_side, (((1,), (1,)), ((), ())), preferred_element_type=jnp.float32
    )


def contract_first(left_side, right_side):
    return lax.dot_general(
        left_side, right_side, (((0,), (0,)), ((), ())), preferred_element_type=jnp.float32
    )


def matmul(left_side, right_side):
    return jnp.dot(left_side, right_side, preferred_element_type=jnp.float32)


def route_slots(idx, experts):
    routes, tok_rows = idx.shape
    names = lax.broadcasted_iota(jnp.int32, (experts, tok_rows), 0)
    members = [(idx[k : k + 1, :] == names).astype(jnp.float32) for k in range(routes)]
    before = (
        lax.broadcasted_iota(jnp.int32, (tok_rows, tok_rows), 0)
        < lax.broadcasted_iota(jnp.int32, (tok_rows, tok_rows), 1)
    ).astype(jnp.bfloat16)
    running = matmul(sum(members).astype(jnp.bfloat16), before)
    return [jnp.sum(running * m, axis=0, keepdims=True).astype(jnp.int32) for m in members]


def slot_masks(idx, experts, low, high):
    routes, tok_rows = idx.shape
    size = high - low
    rows = lax.broadcasted_iota(jnp.int32, (experts * size, tok_rows), 0)
    masks = []
    for k, position in enumerate(route_slots(idx, experts)):
        inside = (position >= low) & (position < high)
        target = jnp.where(inside, idx[k : k + 1, :] * size + position - low, -1)
        masks.append(rows == target)
    return masks


def dispatch_kernel(experts, low, high, idx_ref, prob_ref, tenant_ref, tok_ref, cot_ref, out_ref):
    width = tok_ref.shape[1]
    masks = slot_masks(idx_ref[...], experts, low, high)
    weight = sum(
        jnp.sum(jnp.where(m, prob_ref[k : k + 1, :], 0.0), axis=1, keepdims=True)
        for k, m in enumerate(masks)
    )
    select = sum(m.astype(jnp.float32) for m in masks)
    tenant = jnp.sum(select * tenant_ref[...].astype(jnp.float32), axis=1, keepdims=True)
    out_ref[:, 2 * width :] = jnp.broadcast_to(tenant, (select.shape[0], LANES)).astype(
        jnp.bfloat16
    )
    select = select.astype(jnp.bfloat16)
    step = 512

    def body(i, carry):
        at = pl.multiple_of(i * step, step)
        out_ref[:, pl.ds(at, step)] = matmul(select, tok_ref[:, pl.ds(at, step)]).astype(
            jnp.bfloat16
        )
        out_ref[:, pl.ds(width + at, step)] = (
            matmul(select, cot_ref[:, pl.ds(at, step)]) * weight
        ).astype(jnp.bfloat16)
        return carry

    lax.fori_loop(0, width // step, body, 0)


def dispatch(idx, prob, tenant, tokens, cotangent, experts, low, high):
    tok_rows, width = tokens.shape
    rows = experts * (high - low)
    return pl.pallas_call(
        functools.partial(dispatch_kernel, experts, low, high),
        out_shape=jax.ShapeDtypeStruct((rows, 2 * width + LANES), jnp.bfloat16),
        in_specs=[pl.BlockSpec(memory_space=pltpu.VMEM)] * 5,
        out_specs=pl.BlockSpec(memory_space=pltpu.VMEM),
        compiler_params=pltpu.CompilerParams(vmem_limit_bytes=VMEM_BYTES),
        cost_estimate=pl.CostEstimate(
            flops=4 * rows * tok_rows * width,
            bytes_accessed=4 * tok_rows * width + 4 * rows * width,
            transcendentals=0,
        ),
        name="dispatch",
    )(idx, prob, tenant, tokens, cotangent)


def combine_kernel(experts, idx_ref, *refs):
    out_ref = refs[-1]
    total = None
    for (low, high), ret_ref in zip(CHUNKS, refs):
        masks = slot_masks(idx_ref[...], experts, low, high)
        select = sum(m.astype(jnp.float32) for m in masks).astype(jnp.bfloat16)
        part = contract_first(select, ret_ref[...])
        total = part if total is None else total + part
    out_ref[...] = total.astype(jnp.bfloat16)


def combine(idx, returned, experts):
    tok_rows, width = idx.shape[1], returned[0].shape[1]
    step = 1024
    rows = sum(r.shape[0] for r in returned)
    return pl.pallas_call(
        functools.partial(combine_kernel, experts),
        out_shape=jax.ShapeDtypeStruct((tok_rows, width), jnp.bfloat16),
        grid=(width // step,),
        in_specs=[pl.BlockSpec(idx.shape, lambda i: (0, 0))]
        + [pl.BlockSpec((r.shape[0], step), lambda i: (0, i)) for r in returned],
        out_specs=pl.BlockSpec((tok_rows, step), lambda i: (0, i)),
        compiler_params=pltpu.CompilerParams(vmem_limit_bytes=VMEM_BYTES),
        cost_estimate=pl.CostEstimate(
            flops=2 * rows * tok_rows * width,
            bytes_accessed=2 * (rows + tok_rows) * width,
            transcendentals=0,
        ),
        name="combine",
    )(idx, *returned)


def expert_chunk(received, gate_matrix, up_matrix, down_weight, down_gate, down_up, up_gate, up_up):
    width = gate_matrix.shape[0]
    groups = down_gate.shape[0]
    features = received[:, :width]
    routed = received[:, width : 2 * width]
    tenant = received[:, 2 * width : 2 * width + 1].astype(jnp.int32)
    rank = 16
    selector = (tenant == (jnp.arange(groups, dtype=jnp.int32) // rank)[None, :]).astype(
        jnp.float32
    )
    gate_low = (contract_last(features, down_gate) * selector).astype(jnp.bfloat16)
    up_low = (contract_last(features, down_up) * selector).astype(jnp.bfloat16)
    gate_pre = matmul(features, gate_matrix) + adapter_scale * matmul(gate_low, up_gate)
    up_pre = matmul(features, up_matrix) + adapter_scale * matmul(up_low, up_up)
    back = contract_last(routed, down_weight)
    sig = jax.nn.sigmoid(gate_pre)
    gate_grad = (back * up_pre * (sig + gate_pre * sig * (1.0 - sig))).astype(jnp.bfloat16)
    up_grad = (back * gate_pre * sig).astype(jnp.bfloat16)
    gate_back = (contract_last(gate_grad, up_gate) * selector).astype(jnp.bfloat16)
    up_back = (contract_last(up_grad, up_up) * selector).astype(jnp.bfloat16)
    total = contract_last(gate_grad, gate_matrix) + contract_last(up_grad, up_matrix)
    total = total + adapter_scale * (matmul(gate_back, down_gate) + matmul(up_back, down_up))
    down_part = (contract_first(gate_back, features), contract_first(up_back, features))
    up_part = (contract_first(gate_low, gate_grad), contract_first(up_low, up_grad))
    return total.astype(jnp.bfloat16), down_part, up_part


def reduce_to_owner(part):
    tenants = part.shape[0]
    me = lax.axis_index("dp")
    core, chip = me % 2, me // 2
    chips = tenants // 2
    pairs = part.reshape((chips, 2) + part.shape[1:])
    mine = lax.dynamic_index_in_dim(pairs, core, 1, keepdims=False)
    theirs = lax.dynamic_index_in_dim(pairs, 1 - core, 1, keepdims=False)
    mine = mine + lax.ppermute(theirs, "dp", [(i, i ^ 1) for i in range(tenants)])
    total = lax.dynamic_index_in_dim(mine, chip, 0, keepdims=False)
    for step in range(1, chips):
        sent = lax.dynamic_index_in_dim(mine, (chip + step) % chips, 0, keepdims=False)
        total = total + lax.ppermute(
            sent, "dp", [(i, (i + 2 * step) % tenants) for i in range(tenants)]
        )
    return total


def local(
    tokens,
    cotangent,
    routed_expert_index,
    router_gate_weights,
    token_tenant_index,
    frozen_gate_weight,
    frozen_up_weight,
    frozen_down_weight,
    adapter_down_matrices,
    adapter_up_matrices,
):
    experts = lax.axis_size("expert")
    tenants = lax.axis_size("dp")
    tok_rows, width = tokens.shape
    hidden = frozen_gate_weight.shape[2]
    rank = adapter_down_matrices.shape[3]
    idx = routed_expert_index.T
    prob = router_gate_weights.T
    tenant = token_tenant_index.reshape(1, tok_rows)
    adapters = jnp.concatenate([adapter_down_matrices[0, 0], adapter_up_matrices[0, 0]], axis=-1)
    held = lax.all_gather(adapters, "dp", axis=1, tiled=False)
    held = held.reshape(2, tenants * rank, width + hidden)
    down_gate, down_up = held[0, :, :width], held[1, :, :width]
    up_gate, up_up = held[0, :, width:], held[1, :, width:]
    returned, down_sum, up_sum = [], None, None
    for low, high in CHUNKS:
        sent = dispatch(idx, prob, tenant, tokens, cotangent, experts, low, high)
        received = lax.all_to_all(sent, "expert", split_axis=0, concat_axis=0, tiled=True)
        route_grad, down_part, up_part = expert_chunk(
            received,
            frozen_gate_weight[0],
            frozen_up_weight[0],
            frozen_down_weight[0],
            down_gate,
            down_up,
            up_gate,
            up_up,
        )
        returned.append(
            lax.all_to_all(route_grad, "expert", split_axis=0, concat_axis=0, tiled=True)
        )
        if down_sum is None:
            down_sum, up_sum = down_part, up_part
        else:
            down_sum = tuple(a + b for a, b in zip(down_sum, down_part))
            up_sum = tuple(a + b for a, b in zip(up_sum, up_part))
    down_sum = jnp.concatenate([d.reshape(tenants, rank, width) for d in down_sum], axis=1)
    up_sum = jnp.concatenate([u.reshape(tenants, rank, hidden) for u in up_sum], axis=1)
    owned = adapter_scale * reduce_to_owner(jnp.concatenate([down_sum, up_sum], axis=2))
    down_owned = owned[:, :width].reshape(1, 1, 2, rank, width)
    up_owned = owned[:, width:].reshape(1, 1, 2, rank, hidden)
    token_grads = combine(idx, returned, experts)
    return token_grads, down_owned, up_owned


def solution(mesh):
    in_specs = (
        P(("dp", "expert"), None),
        P(("dp", "expert"), None),
        P(("dp", "expert"), None),
        P(("dp", "expert"), None),
        P(("dp", "expert")),
        P("expert", None, None),
        P("expert", None, None),
        P("expert", None, None),
        P("dp", "expert", None, None, None),
        P("dp", "expert", None, None, None),
    )
    out_specs = (
        P(("dp", "expert"), None),
        P("dp", "expert", None, None, None),
        P("dp", "expert", None, None, None),
    )
    return jax.shard_map(local, mesh=mesh, in_specs=in_specs, out_specs=out_specs, check_vma=False)
```

```python
import functools

import jax
import jax.numpy as jnp
from jax import lax
from jax.experimental import pallas as pl
from jax.experimental.pallas import tpu as pltpu
from jax.sharding import PartitionSpec as P

adapter_scale = 0.5
LANES = 128
VMEM_BYTES = 60 * 1024 * 1024


def contract_last(left_side, right_side):
    return lax.dot_general(
        left_side, right_side, (((1,), (1,)), ((), ())), preferred_element_type=jnp.float32
    )


def matmul(left_side, right_side):
    return jnp.dot(left_side, right_side, preferred_element_type=jnp.float32)


def slot_masks(idx, experts, capacity):
    routes, tok_rows = idx.shape
    names = lax.broadcasted_iota(jnp.int32, (experts, tok_rows), 0)
    members = [(idx[k : k + 1, :] == names).astype(jnp.float32) for k in range(routes)]
    before = (
        lax.broadcasted_iota(jnp.int32, (tok_rows, tok_rows), 0)
        < lax.broadcasted_iota(jnp.int32, (tok_rows, tok_rows), 1)
    ).astype(jnp.bfloat16)
    running = matmul(sum(members).astype(jnp.bfloat16), before)
    rows = lax.broadcasted_iota(jnp.int32, (experts * capacity, tok_rows), 0)
    masks = []
    for k, member in enumerate(members):
        position = jnp.sum(running * member, axis=0, keepdims=True).astype(jnp.int32)
        masks.append(rows == idx[k : k + 1, :] * capacity + position)
    return masks


def dispatch_kernel(
    experts,
    capacity,
    idx_ref,
    prob_ref,
    tenant_ref,
    tok_ref,
    cot_ref,
    out_ref,
    select,
    weight,
    tenant_rows,
    feat_out,
    cot_out,
    sems,
    tenant_sem,
):
    step = pl.program_id(0)
    steps = pl.num_programs(0)
    block = tok_ref.shape[1]
    width = block * steps
    slot = lax.rem(step, 2)

    def copies(at, slot):
        column = pl.multiple_of(at * block, block)
        return (
            pltpu.make_async_copy(
                feat_out.at[slot], out_ref.at[:, pl.ds(column, block)], sems.at[0, slot]
            ),
            pltpu.make_async_copy(
                cot_out.at[slot], out_ref.at[:, pl.ds(width + column, block)], sems.at[1, slot]
            ),
        )

    tenant_copy = pltpu.make_async_copy(
        tenant_rows, out_ref.at[:, pl.ds(2 * width, LANES)], tenant_sem
    )

    @pl.when(step == 0)
    def _():
        masks = slot_masks(idx_ref[...], experts, capacity)
        filled = sum(m.astype(jnp.float32) for m in masks)
        weight[...] = sum(
            jnp.sum(jnp.where(m, prob_ref[k : k + 1, :], 0.0), axis=1, keepdims=True)
            for k, m in enumerate(masks)
        )
        tenant = jnp.sum(filled * tenant_ref[...].astype(jnp.float32), axis=1, keepdims=True)
        tenant_rows[...] = jnp.broadcast_to(tenant, tenant_rows.shape).astype(jnp.bfloat16)
        tenant_copy.start()
        select[...] = filled.astype(jnp.bfloat16)

    @pl.when(step >= 2)
    def _():
        for copy in copies(step - 2, slot):
            copy.wait()

    feat_out[slot] = matmul(select[...], tok_ref[...]).astype(jnp.bfloat16)
    cot_out[slot] = (matmul(select[...], cot_ref[...]) * weight[...]).astype(jnp.bfloat16)
    for copy in copies(step, slot):
        copy.start()

    @pl.when(step == steps - 1)
    def _():
        for copy in copies(step - 1, 1 - slot):
            copy.wait()
        for copy in copies(step, slot):
            copy.wait()
        tenant_copy.wait()


def dispatch(idx, prob, tenant, tokens, cotangent, experts, capacity):
    tok_rows, width = tokens.shape
    rows = experts * capacity
    block = 512
    return pl.pallas_call(
        functools.partial(dispatch_kernel, experts, capacity),
        out_shape=jax.ShapeDtypeStruct((rows, 2 * width + LANES), jnp.bfloat16),
        grid=(width // block,),
        in_specs=[
            pl.BlockSpec(idx.shape, lambda i: (0, 0)),
            pl.BlockSpec(prob.shape, lambda i: (0, 0)),
            pl.BlockSpec(tenant.shape, lambda i: (0, 0)),
            pl.BlockSpec((tok_rows, block), lambda i: (0, i)),
            pl.BlockSpec((tok_rows, block), lambda i: (0, i)),
        ],
        out_specs=pl.BlockSpec(memory_space=pl.ANY),
        scratch_shapes=[
            pltpu.VMEM((rows, tok_rows), jnp.bfloat16),
            pltpu.VMEM((rows, 1), jnp.float32),
            pltpu.VMEM((rows, LANES), jnp.bfloat16),
            pltpu.VMEM((2, rows, block), jnp.bfloat16),
            pltpu.VMEM((2, rows, block), jnp.bfloat16),
            pltpu.SemaphoreType.DMA((2, 2)),
            pltpu.SemaphoreType.DMA,
        ],
        compiler_params=pltpu.CompilerParams(vmem_limit_bytes=VMEM_BYTES),
        cost_estimate=pl.CostEstimate(
            flops=4 * rows * tok_rows * width,
            bytes_accessed=4 * tok_rows * width + 4 * rows * width,
            transcendentals=0,
        ),
        name="dispatch",
    )(idx, prob, tenant, tokens, cotangent)


def combine_kernel(experts, capacity, idx_ref, ret_ref, out_ref, select):
    @pl.when(pl.program_id(0) == 0)
    def _():
        filled = sum(m.astype(jnp.float32) for m in slot_masks(idx_ref[...], experts, capacity))
        select[...] = filled.T.astype(jnp.bfloat16)

    out_ref[...] = matmul(select[...], ret_ref[...]).astype(jnp.bfloat16)


def combine(idx, returned, experts, capacity):
    tok_rows, width = idx.shape[1], returned.shape[1]
    block = 512
    rows = returned.shape[0]
    return pl.pallas_call(
        functools.partial(combine_kernel, experts, capacity),
        out_shape=jax.ShapeDtypeStruct((tok_rows, width), jnp.bfloat16),
        grid=(width // block,),
        in_specs=[
            pl.BlockSpec(idx.shape, lambda i: (0, 0)),
            pl.BlockSpec((rows, block), lambda i: (0, i)),
        ],
        out_specs=pl.BlockSpec((tok_rows, block), lambda i: (0, i)),
        scratch_shapes=[pltpu.VMEM((tok_rows, rows), jnp.bfloat16)],
        compiler_params=pltpu.CompilerParams(vmem_limit_bytes=VMEM_BYTES),
        cost_estimate=pl.CostEstimate(
            flops=2 * rows * tok_rows * width,
            bytes_accessed=2 * (rows + tok_rows) * width,
            transcendentals=0,
        ),
        name="combine",
    )(idx, returned)


def expert_kernel(
    rank,
    got_ref,
    held_ref,
    gate_ref,
    up_ref,
    down_ref,
    route_out,
    part_out,
    feat,
    cot,
    tenant,
    low_held,
    high_held,
    gate,
    up,
    down,
    grads,
    down_sum,
    up_sum,
    gate_pre,
    up_pre,
    sems,
    out_sems,
):
    width = feat.shape[1]
    hidden = down.shape[0]
    groups = held_ref.shape[0]
    block = 256
    step = 512
    parts = hidden // block

    stages = (
        (
            (got_ref.at[:, pl.ds(2 * width, LANES)], tenant),
            (got_ref.at[:, pl.ds(0, width)], feat),
            (held_ref.at[:, pl.ds(0, width)], low_held),
        ),
        ((gate_ref, gate), (held_ref.at[:, pl.ds(width, hidden)], high_held)),
        ((up_ref, up),),
        ((got_ref.at[:, pl.ds(width, width)], cot), (down_ref, down)),
    )
    copies = []
    for stage in stages:
        first = sum(len(c) for c in copies)
        copies.append(
            [
                pltpu.make_async_copy(source, target, sems.at[first + i])
                for i, (source, target) in enumerate(stage)
            ]
        )
    ahead = 2
    for stage in copies[:ahead]:
        for copy in stage:
            copy.start()

    def arrive(i):
        for copy in copies[i]:
            copy.wait()
        if i + ahead < len(copies):
            for copy in copies[i + ahead]:
                copy.start()

    arrive(0)
    owner = lax.broadcasted_iota(jnp.int32, (1, groups), 1) // (2 * rank)
    selector = (tenant[:, 0:1].astype(jnp.int32) == owner).astype(jnp.float32)
    low = (contract_last(feat[...], low_held[...]) * selector).astype(jnp.bfloat16)
    arrive(1)
    is_gate = lax.broadcasted_iota(jnp.int32, (groups, 1), 0) // rank % 2 == 0
    high = high_held[...].astype(jnp.float32)
    high_gate = jnp.where(is_gate, high, 0.0).astype(jnp.bfloat16)
    high_up = jnp.where(is_gate, 0.0, high).astype(jnp.bfloat16)
    for h in range(parts):
        at = slice(h * block, (h + 1) * block)
        gate_pre[:, at] = matmul(feat[...], gate[:, at]) + adapter_scale * matmul(
            low, high_gate[:, at]
        )
    arrive(2)
    for h in range(parts):
        at = slice(h * block, (h + 1) * block)
        up_pre[:, at] = matmul(feat[...], up[:, at]) + adapter_scale * matmul(low, high_up[:, at])
    arrive(3)
    for h in range(parts):
        at = slice(h * block, (h + 1) * block)
        after = slice(hidden + h * block, hidden + (h + 1) * block)
        back = contract_last(cot[...], down[at])
        pre = gate_pre[:, at]
        sig = jax.nn.sigmoid(pre)
        grads[:, at] = (back * up_pre[:, at] * (sig + pre * sig * (1.0 - sig))).astype(jnp.bfloat16)
        grads[:, after] = (back * pre * sig).astype(jnp.bfloat16)
    low_back = contract_last(grads[:, :hidden], high_gate) + contract_last(
        grads[:, hidden:], high_up
    )
    low_back = (low_back * selector).astype(jnp.bfloat16)
    back_t = low_back.astype(jnp.float32).T.astype(jnp.bfloat16)
    low_t = low.astype(jnp.float32).T.astype(jnp.bfloat16)
    up_sum[...] = adapter_scale * jnp.where(
        is_gate, matmul(low_t, grads[:, :hidden]), matmul(low_t, grads[:, hidden:])
    )
    leaving = [
        pltpu.make_async_copy(up_sum, part_out.at[:, pl.ds(width, hidden)], out_sems.at[0])
    ]
    leaving[-1].start()
    for i in range(width // step):
        at = pl.ds(i * step, step)
        down_sum[:, at] = adapter_scale * matmul(back_t, feat[:, at])
        leaving.append(
            pltpu.make_async_copy(down_sum.at[:, at], part_out.at[:, at], out_sems.at[len(leaving)])
        )
        leaving[-1].start()
    for i in range(width // step):
        at = pl.ds(i * step, step)
        cot[:, at] = (
            contract_last(grads[:, :hidden], gate[at])
            + contract_last(grads[:, hidden:], up[at])
            + adapter_scale * matmul(low_back, low_held[:, at])
        ).astype(jnp.bfloat16)
        leaving.append(
            pltpu.make_async_copy(cot.at[:, at], route_out.at[:, at], out_sems.at[len(leaving)])
        )
        leaving[-1].start()
    for copy in leaving:
        copy.wait()


def expert_pass(received, held, gate_matrix, up_matrix, down_weight, rank):
    rows = received.shape[0]
    width, hidden = gate_matrix.shape
    groups = held.shape[0]
    anywhere = pl.BlockSpec(memory_space=pl.ANY)
    return pl.pallas_call(
        functools.partial(expert_kernel, rank),
        out_shape=(
            jax.ShapeDtypeStruct((rows, width), jnp.bfloat16),
            jax.ShapeDtypeStruct((groups, width + hidden), jnp.float32),
        ),
        in_specs=[anywhere] * 5,
        out_specs=(anywhere, anywhere),
        scratch_shapes=[
            pltpu.VMEM((rows, width), jnp.bfloat16),
            pltpu.VMEM((rows, width), jnp.bfloat16),
            pltpu.VMEM((rows, LANES), jnp.bfloat16),
            pltpu.VMEM((groups, width), jnp.bfloat16),
            pltpu.VMEM((groups, hidden), jnp.bfloat16),
            pltpu.VMEM((width, hidden), jnp.bfloat16),
            pltpu.VMEM((width, hidden), jnp.bfloat16),
            pltpu.VMEM((hidden, width), jnp.bfloat16),
            pltpu.VMEM((rows, 2 * hidden), jnp.bfloat16),
            pltpu.VMEM((groups, width), jnp.float32),
            pltpu.VMEM((groups, hidden), jnp.float32),
            pltpu.VMEM((rows, hidden), jnp.float32),
            pltpu.VMEM((rows, hidden), jnp.float32),
            pltpu.SemaphoreType.DMA((8,)),
            pltpu.SemaphoreType.DMA((1 + 2 * (width // 512),)),
        ],
        compiler_params=pltpu.CompilerParams(vmem_limit_bytes=VMEM_BYTES),
        cost_estimate=pl.CostEstimate(
            flops=10 * rows * width * hidden + 6 * rows * width * groups,
            bytes_accessed=6 * width * hidden + 6 * rows * width,
            transcendentals=rows * hidden,
        ),
        name="expert_pass",
    )(received, held, gate_matrix, up_matrix, down_weight)


def chip_sums(part):
    chips = part.shape[0]
    devices = lax.axis_size("dp")
    per_chip = devices // chips
    chip = lax.axis_index("dp") // per_chip
    own = lax.dynamic_index_in_dim(part, chip, 0, keepdims=False)
    arrived = []
    for step in range(1, chips):
        sent = lax.dynamic_index_in_dim(part, (chip + step) % chips, 0, keepdims=False)
        arrived.append(
            lax.ppermute(
                sent, "dp", [(i, (i + per_chip * step) % devices) for i in range(devices)]
            )
        )
    return own, arrived


def exchange(named, rows):
    return lax.cond(
        named,
        lambda r: lax.all_to_all(r, "expert", split_axis=0, concat_axis=0, tiled=True),
        jnp.zeros_like,
        rows,
    )


def local(
    tokens,
    cotangent,
    routed_expert_index,
    router_gate_weights,
    token_tenant_index,
    frozen_gate_weight,
    frozen_up_weight,
    frozen_down_weight,
    adapter_down_matrices,
    adapter_up_matrices,
):
    experts = lax.axis_size("expert")
    tenants = lax.axis_size("dp")
    tok_rows, width = tokens.shape
    routes = routed_expert_index.shape[1]
    hidden = frozen_gate_weight.shape[2]
    rank = adapter_down_matrices.shape[3]
    groups = tenants * rank
    capacity = 5 * tok_rows * routes // (4 * experts)
    idx = routed_expert_index.T
    prob = router_gate_weights.T
    tenant = token_tenant_index.reshape(1, tok_rows)
    adapters = jnp.concatenate([adapter_down_matrices[0, 0], adapter_up_matrices[0, 0]], axis=-1)
    held = lax.all_gather(adapters, "dp", axis=0, tiled=True)
    sent = dispatch(idx, prob, tenant, tokens, cotangent, experts, capacity)
    named = routed_expert_index[0, 0] >= 0
    received = exchange(named, sent)
    received, held = lax.optimization_barrier((received, held))
    route_grad, part = expert_pass(
        received,
        held.reshape(2 * groups, width + hidden),
        frozen_gate_weight[0],
        frozen_up_weight[0],
        frozen_down_weight[0],
        rank,
    )
    own, arrived = chip_sums(part.reshape(tenants // 2, 4 * rank, width + hidden))
    returned = exchange(named, route_grad)
    returned, own, *arrived = lax.optimization_barrier((returned, own, *arrived))
    token_grads = combine(idx, returned, experts, capacity)
    total = sum(arrived, own).reshape(2, 2 * rank, width + hidden)
    core = lax.axis_index("dp") % 2
    theirs = lax.dynamic_index_in_dim(total, 1 - core, 0, keepdims=False)
    owned = lax.dynamic_index_in_dim(total, core, 0, keepdims=False) + lax.ppermute(
        theirs, "dp", [(i, i ^ 1) for i in range(tenants)]
    )
    down_owned = owned[:, :width].reshape(1, 1, 2, rank, width)
    up_owned = owned[:, width:].reshape(1, 1, 2, rank, hidden)
    return token_grads, down_owned, up_owned


def solution(mesh):
    in_specs = (
        P(("dp", "expert"), None),
        P(("dp", "expert"), None),
        P(("dp", "expert"), None),
        P(("dp", "expert"), None),
        P(("dp", "expert")),
        P("expert", None, None),
        P("expert", None, None),
        P("expert", None, None),
        P("dp", "expert", None, None, None),
        P("dp", "expert", None, None, None),
    )
    out_specs = (
        P(("dp", "expert"), None),
        P("dp", "expert", None, None, None),
        P("dp", "expert", None, None, None),
    )
    return jax.shard_map(local, mesh=mesh, in_specs=in_specs, out_specs=out_specs, check_vma=False)
```

```python
import functools

import jax
import jax.numpy as jnp
from jax import lax
from jax.experimental import pallas as pl
from jax.experimental.pallas import tpu as pltpu
from jax.sharding import PartitionSpec as P

adapter_scale = 0.5
LANES = 128
VMEM_BYTES = 60 * 1024 * 1024


def contract_last(left_side, right_side):
    return lax.dot_general(
        left_side, right_side, (((1,), (1,)), ((), ())), preferred_element_type=jnp.float32
    )


def matmul(left_side, right_side):
    return jnp.dot(left_side, right_side, preferred_element_type=jnp.float32)


def route_slots(idx, experts, capacity):
    routes, tok_rows = idx.shape
    names = lax.broadcasted_iota(jnp.int32, (experts, tok_rows), 0)
    members = [(idx[k : k + 1, :] == names).astype(jnp.float32) for k in range(routes)]
    before = (
        lax.broadcasted_iota(jnp.int32, (tok_rows, tok_rows), 0)
        < lax.broadcasted_iota(jnp.int32, (tok_rows, tok_rows), 1)
    ).astype(jnp.bfloat16)
    running = matmul(sum(members).astype(jnp.bfloat16), before)
    return [
        idx[k : k + 1, :] * capacity
        + jnp.sum(running * member, axis=0, keepdims=True).astype(jnp.int32)
        for k, member in enumerate(members)
    ]


def dispatch_kernel(
    experts,
    capacity,
    idx_ref,
    prob_ref,
    tenant_ref,
    tok_ref,
    cot_ref,
    out_ref,
    select,
    weight,
    tenant_rows,
    feat_out,
    cot_out,
    sems,
    tenant_sem,
):
    step = pl.program_id(0)
    steps = pl.num_programs(0)
    block = tok_ref.shape[1]
    width = block * steps
    slot = lax.rem(step, 2)

    def copies(at, slot):
        column = pl.multiple_of(at * block, block)
        return (
            pltpu.make_async_copy(
                feat_out.at[slot], out_ref.at[:, pl.ds(column, block)], sems.at[0, slot]
            ),
            pltpu.make_async_copy(
                cot_out.at[slot], out_ref.at[:, pl.ds(width + column, block)], sems.at[1, slot]
            ),
        )

    tenant_copy = pltpu.make_async_copy(
        tenant_rows, out_ref.at[:, pl.ds(2 * width, LANES)], tenant_sem
    )

    @pl.when(step == 0)
    def _():
        rows = lax.broadcasted_iota(jnp.int32, select.shape, 0)
        masks = [rows == slots for slots in route_slots(idx_ref[...], experts, capacity)]
        filled = sum(m.astype(jnp.float32) for m in masks)
        weight[...] = sum(
            jnp.sum(jnp.where(m, prob_ref[k : k + 1, :], 0.0), axis=1, keepdims=True)
            for k, m in enumerate(masks)
        )
        tenant = jnp.sum(filled * tenant_ref[...].astype(jnp.float32), axis=1, keepdims=True)
        tenant_rows[...] = jnp.broadcast_to(tenant, tenant_rows.shape).astype(jnp.bfloat16)
        tenant_copy.start()
        select[...] = filled.astype(jnp.bfloat16)

    @pl.when(step >= 2)
    def _():
        for copy in copies(step - 2, slot):
            copy.wait()

    feat_out[slot] = matmul(select[...], tok_ref[...]).astype(jnp.bfloat16)
    cot_out[slot] = (matmul(select[...], cot_ref[...]) * weight[...]).astype(jnp.bfloat16)
    for copy in copies(step, slot):
        copy.start()

    @pl.when(step == steps - 1)
    def _():
        for copy in copies(step - 1, 1 - slot):
            copy.wait()
        for copy in copies(step, slot):
            copy.wait()
        tenant_copy.wait()


def dispatch(idx, prob, tenant, tokens, cotangent, experts, capacity):
    tok_rows, width = tokens.shape
    rows = experts * capacity
    block = 512
    return pl.pallas_call(
        functools.partial(dispatch_kernel, experts, capacity),
        out_shape=jax.ShapeDtypeStruct((rows, 2 * width + LANES), jnp.bfloat16),
        grid=(width // block,),
        in_specs=[
            pl.BlockSpec(idx.shape, lambda i: (0, 0)),
            pl.BlockSpec(prob.shape, lambda i: (0, 0)),
            pl.BlockSpec(tenant.shape, lambda i: (0, 0)),
            pl.BlockSpec((tok_rows, block), lambda i: (0, i)),
            pl.BlockSpec((tok_rows, block), lambda i: (0, i)),
        ],
        out_specs=pl.BlockSpec(memory_space=pl.ANY),
        scratch_shapes=[
            pltpu.VMEM((rows, tok_rows), jnp.bfloat16),
            pltpu.VMEM((rows, 1), jnp.float32),
            pltpu.VMEM((rows, LANES), jnp.bfloat16),
            pltpu.VMEM((2, rows, block), jnp.bfloat16),
            pltpu.VMEM((2, rows, block), jnp.bfloat16),
            pltpu.SemaphoreType.DMA((2, 2)),
            pltpu.SemaphoreType.DMA,
        ],
        compiler_params=pltpu.CompilerParams(vmem_limit_bytes=VMEM_BYTES),
        cost_estimate=pl.CostEstimate(
            flops=4 * rows * tok_rows * width,
            bytes_accessed=4 * tok_rows * width + 4 * rows * width,
            transcendentals=0,
        ),
        name="dispatch",
    )(idx, prob, tenant, tokens, cotangent)


def combine_kernel(experts, capacity, idx_ref, ret_ref, out_ref, select):
    @pl.when(pl.program_id(0) == 0)
    def _():
        slots = route_slots(idx_ref[...], experts, capacity)
        rows = lax.broadcasted_iota(jnp.int32, (8, slots[0].shape[1]), 0)
        table = sum(jnp.where(rows == k, s.astype(jnp.float32), 0.0) for k, s in enumerate(slots))
        table = table.T.astype(jnp.int32)
        lanes = lax.broadcasted_iota(jnp.int32, select.shape, 1)
        select[...] = sum(
            (lanes == table[:, k : k + 1]).astype(jnp.float32) for k in range(len(slots))
        ).astype(jnp.bfloat16)

    out_ref[...] = matmul(select[...], ret_ref[...]).astype(jnp.bfloat16)


def combine(idx, returned, experts, capacity):
    tok_rows, width = idx.shape[1], returned.shape[1]
    block = 1024
    rows = returned.shape[0]
    return pl.pallas_call(
        functools.partial(combine_kernel, experts, capacity),
        out_shape=jax.ShapeDtypeStruct((tok_rows, width), jnp.bfloat16),
        grid=(width // block,),
        in_specs=[
            pl.BlockSpec(idx.shape, lambda i: (0, 0)),
            pl.BlockSpec((rows, block), lambda i: (0, i)),
        ],
        out_specs=pl.BlockSpec((tok_rows, block), lambda i: (0, i)),
        scratch_shapes=[pltpu.VMEM((tok_rows, rows), jnp.bfloat16)],
        compiler_params=pltpu.CompilerParams(vmem_limit_bytes=VMEM_BYTES),
        cost_estimate=pl.CostEstimate(
            flops=2 * rows * tok_rows * width,
            bytes_accessed=2 * (rows + tok_rows) * width,
            transcendentals=0,
        ),
        name="combine",
    )(idx, returned)


def expert_kernel(
    rank,
    chips,
    got_ref,
    gate_ref,
    up_ref,
    down_ref,
    *refs,
):
    held_refs, route_out, part_outs = refs[:chips], refs[chips], refs[chips + 1 : 2 * chips + 1]
    expert_body(rank, got_ref, gate_ref, up_ref, down_ref, held_refs, route_out, part_outs, *refs[2 * chips + 1 :])


def expert_body(
    rank,
    got_ref,
    gate_ref,
    up_ref,
    down_ref,
    held_refs,
    route_out,
    part_outs,
    feat,
    cot,
    tenant,
    low_held,
    high_held,
    gate,
    up,
    down,
    grads,
    down_sum,
    up_sum,
    gate_pre,
    up_pre,
    sems,
    out_sems,
):
    width = feat.shape[1]
    hidden = down.shape[0]
    groups, chip_rows = low_held.shape[0], held_refs[0].shape[0]
    block = 256
    step = 512
    parts = hidden // block

    stages = (
        (
            (got_ref.at[:, pl.ds(2 * width, LANES)], tenant),
            (got_ref.at[:, pl.ds(0, width)], feat),
            *(
                (held.at[:, pl.ds(0, width)], low_held.at[pl.ds(c * chip_rows, chip_rows)])
                for c, held in enumerate(held_refs)
            ),
        ),
        (
            (gate_ref, gate),
            *(
                (held.at[:, pl.ds(width, hidden)], high_held.at[pl.ds(c * chip_rows, chip_rows)])
                for c, held in enumerate(held_refs)
            ),
        ),
        ((up_ref, up),),
        ((got_ref.at[:, pl.ds(width, width)], cot), (down_ref, down)),
    )
    copies = []
    for stage in stages:
        first = sum(len(c) for c in copies)
        copies.append(
            [
                pltpu.make_async_copy(source, target, sems.at[first + i])
                for i, (source, target) in enumerate(stage)
            ]
        )
    ahead = 2
    for stage in copies[:ahead]:
        for copy in stage:
            copy.start()

    def arrive(i):
        for copy in copies[i]:
            copy.wait()
        if i + ahead < len(copies):
            for copy in copies[i + ahead]:
                copy.start()

    arrive(0)
    owner = lax.broadcasted_iota(jnp.int32, (1, groups), 1) // (2 * rank)
    selector = (tenant[:, 0:1].astype(jnp.int32) == owner).astype(jnp.float32)
    low = (contract_last(feat[...], low_held[...]) * selector).astype(jnp.bfloat16)
    arrive(1)
    is_gate = lax.broadcasted_iota(jnp.int32, (groups, 1), 0) // rank % 2 == 0
    high = high_held[...].astype(jnp.float32)
    high_gate = jnp.where(is_gate, high, 0.0).astype(jnp.bfloat16)
    high_up = jnp.where(is_gate, 0.0, high).astype(jnp.bfloat16)
    for h in range(parts):
        at = slice(h * block, (h + 1) * block)
        gate_pre[:, at] = matmul(feat[...], gate[:, at]) + adapter_scale * matmul(
            low, high_gate[:, at]
        )
    arrive(2)
    for h in range(parts):
        at = slice(h * block, (h + 1) * block)
        up_pre[:, at] = matmul(feat[...], up[:, at]) + adapter_scale * matmul(low, high_up[:, at])
    arrive(3)
    for h in range(parts):
        at = slice(h * block, (h + 1) * block)
        after = slice(hidden + h * block, hidden + (h + 1) * block)
        back = contract_last(cot[...], down[at])
        pre = gate_pre[:, at]
        sig = jax.nn.sigmoid(pre)
        grads[:, at] = (back * up_pre[:, at] * (sig + pre * sig * (1.0 - sig))).astype(jnp.bfloat16)
        grads[:, after] = (back * pre * sig).astype(jnp.bfloat16)
    low_back = contract_last(grads[:, :hidden], high_gate) + contract_last(
        grads[:, hidden:], high_up
    )
    low_back = (low_back * selector).astype(jnp.bfloat16)
    back_t = low_back.astype(jnp.float32).T.astype(jnp.bfloat16)
    low_t = low.astype(jnp.float32).T.astype(jnp.bfloat16)
    up_sum[...] = adapter_scale * jnp.where(
        is_gate, matmul(low_t, grads[:, :hidden]), matmul(low_t, grads[:, hidden:])
    )
    leaving = []

    def leave(source, target):
        leaving.append(pltpu.make_async_copy(source, target, out_sems.at[len(leaving)]))
        leaving[-1].start()

    for c, part_out in enumerate(part_outs):
        leave(up_sum.at[pl.ds(c * chip_rows, chip_rows)], part_out.at[:, pl.ds(width, hidden)])
    for i in range(width // step):
        at = pl.ds(i * step, step)
        down_sum[:, at] = adapter_scale * matmul(back_t, feat[:, at])
    for c, part_out in enumerate(part_outs):
        leave(down_sum.at[pl.ds(c * chip_rows, chip_rows)], part_out.at[:, pl.ds(0, width)])
    for i in range(width // step):
        at = pl.ds(i * step, step)
        cot[:, at] = (
            contract_last(grads[:, :hidden], gate[at])
            + contract_last(grads[:, hidden:], up[at])
            + adapter_scale * matmul(low_back, low_held[:, at])
        ).astype(jnp.bfloat16)
        leave(cot.at[:, at], route_out.at[:, at])
    for copy in leaving:
        copy.wait()


def expert_pass(received, gate_matrix, up_matrix, down_weight, held, rank):
    rows = received.shape[0]
    width, hidden = gate_matrix.shape
    chips, chip_rows = len(held), held[0].shape[0]
    groups = chips * chip_rows
    anywhere = pl.BlockSpec(memory_space=pl.ANY)
    return pl.pallas_call(
        functools.partial(expert_kernel, rank, chips),
        out_shape=(
            jax.ShapeDtypeStruct((rows, width), jnp.bfloat16),
            *[jax.ShapeDtypeStruct((chip_rows, width + hidden), jnp.float32)] * chips,
        ),
        in_specs=[anywhere] * (4 + chips),
        out_specs=(anywhere,) * (1 + chips),
        scratch_shapes=[
            pltpu.VMEM((rows, width), jnp.bfloat16),
            pltpu.VMEM((rows, width), jnp.bfloat16),
            pltpu.VMEM((rows, LANES), jnp.bfloat16),
            pltpu.VMEM((groups, width), jnp.bfloat16),
            pltpu.VMEM((groups, hidden), jnp.bfloat16),
            pltpu.VMEM((width, hidden), jnp.bfloat16),
            pltpu.VMEM((width, hidden), jnp.bfloat16),
            pltpu.VMEM((hidden, width), jnp.bfloat16),
            pltpu.VMEM((rows, 2 * hidden), jnp.bfloat16),
            pltpu.VMEM((groups, width), jnp.float32),
            pltpu.VMEM((groups, hidden), jnp.float32),
            pltpu.VMEM((rows, hidden), jnp.float32),
            pltpu.VMEM((rows, hidden), jnp.float32),
            pltpu.SemaphoreType.DMA((6 + 2 * chips,)),
            pltpu.SemaphoreType.DMA((2 * chips + width // 512,)),
        ],
        compiler_params=pltpu.CompilerParams(vmem_limit_bytes=VMEM_BYTES),
        cost_estimate=pl.CostEstimate(
            flops=10 * rows * width * hidden + 6 * rows * width * groups,
            bytes_accessed=6 * width * hidden + 6 * rows * width,
            transcendentals=rows * hidden,
        ),
        name="expert_pass",
    )(received, gate_matrix, up_matrix, down_weight, *held)


def along_x(rows, step):
    devices = lax.axis_size("dp")
    return lax.ppermute(rows, "dp", [(i, (i + 2 * step) % devices) for i in range(devices)])


def other_core(rows):
    return lax.ppermute(rows, "dp", [(i, i ^ 1) for i in range(lax.axis_size("dp"))])


def exchange(named, rows):
    return lax.cond(
        named,
        lambda r: lax.all_to_all(r, "expert", split_axis=0, concat_axis=0, tiled=True),
        jnp.zeros_like,
        rows,
    )


def local(
    tokens,
    cotangent,
    routed_expert_index,
    router_gate_weights,
    token_tenant_index,
    frozen_gate_weight,
    frozen_up_weight,
    frozen_down_weight,
    adapter_down_matrices,
    adapter_up_matrices,
):
    experts = lax.axis_size("expert")
    tenants = lax.axis_size("dp")
    tok_rows, width = tokens.shape
    routes = routed_expert_index.shape[1]
    hidden = frozen_gate_weight.shape[2]
    rank = adapter_down_matrices.shape[3]
    capacity = 5 * tok_rows * routes // (4 * experts)
    idx = routed_expert_index.T
    prob = router_gate_weights.T
    me = lax.axis_index("dp")
    chips = tenants // 2
    tenant = (me // 2 - token_tenant_index // 2) % chips * 2 + (me + token_tenant_index) % 2
    tenant = tenant.reshape(1, tok_rows)
    adapters = jnp.concatenate([adapter_down_matrices[0, 0], adapter_up_matrices[0, 0]], axis=-1)
    adapters = adapters.reshape(2 * rank, width + hidden)
    pair = jnp.concatenate([adapters, other_core(adapters)], axis=0)
    held = [pair] + [along_x(pair, step) for step in range(1, chips)]
    named = me < tenants
    sent = dispatch(idx, prob, tenant, tokens, cotangent, experts, capacity)
    received = exchange(named, sent)
    received, *held = lax.optimization_barrier((received, *held))
    route_grad, own, *parts = expert_pass(
        received,
        frozen_gate_weight[0],
        frozen_up_weight[0],
        frozen_down_weight[0],
        held,
        rank,
    )
    arrived = [along_x(part, -step) for step, part in enumerate(parts, 1)]
    returned = exchange(named, route_grad)
    returned, own, *arrived = lax.optimization_barrier((returned, own, *arrived))
    token_grads = combine(idx, returned, experts, capacity)
    total = sum(arrived, own)
    owned = total[: 2 * rank] + other_core(total[2 * rank :])
    down_owned = owned[:, :width].reshape(1, 1, 2, rank, width)
    up_owned = owned[:, width:].reshape(1, 1, 2, rank, hidden)
    return token_grads, down_owned, up_owned


def solution(mesh):
    in_specs = (
        P(("dp", "expert"), None),
        P(("dp", "expert"), None),
        P(("dp", "expert"), None),
        P(("dp", "expert"), None),
        P(("dp", "expert")),
        P("expert", None, None),
        P("expert", None, None),
        P("expert", None, None),
        P("dp", "expert", None, None, None),
        P("dp", "expert", None, None, None),
    )
    out_specs = (
        P(("dp", "expert"), None),
        P("dp", "expert", None, None, None),
        P("dp", "expert", None, None, None),
    )
    return jax.shard_map(local, mesh=mesh, in_specs=in_specs, out_specs=out_specs, check_vma=False)
```

```python
import functools

import jax
import jax.numpy as jnp
from jax import lax
from jax.experimental import pallas as pl
from jax.experimental.pallas import tpu as pltpu
from jax.sharding import PartitionSpec as P

adapter_scale = 0.5
LANES = 128
VMEM_BYTES = 60 * 1024 * 1024


def contract_last(left_side, right_side):
    return lax.dot_general(
        left_side, right_side, (((1,), (1,)), ((), ())), preferred_element_type=jnp.float32
    )


def matmul(left_side, right_side):
    return jnp.dot(left_side, right_side, preferred_element_type=jnp.float32)


def route_slots(idx, experts, capacity):
    routes, tok_rows = idx.shape
    names = lax.broadcasted_iota(jnp.int32, (experts, tok_rows), 0)
    members = [(idx[k : k + 1, :] == names).astype(jnp.float32) for k in range(routes)]
    before = (
        lax.broadcasted_iota(jnp.int32, (tok_rows, tok_rows), 0)
        < lax.broadcasted_iota(jnp.int32, (tok_rows, tok_rows), 1)
    ).astype(jnp.bfloat16)
    running = matmul(sum(members).astype(jnp.bfloat16), before)
    return [
        idx[k : k + 1, :] * capacity
        + jnp.sum(running * member, axis=0, keepdims=True).astype(jnp.int32)
        for k, member in enumerate(members)
    ]


def dispatch_kernel(
    experts,
    capacity,
    idx_ref,
    prob_ref,
    tenant_ref,
    tok_ref,
    cot_ref,
    out_ref,
    select,
    weight,
    tenant_rows,
    feat_out,
    cot_out,
    sems,
    tenant_sem,
):
    step = pl.program_id(0)
    steps = pl.num_programs(0)
    block = tok_ref.shape[1]
    width = block * steps
    slot = lax.rem(step, 2)

    def copies(at, slot):
        column = pl.multiple_of(at * block, block)
        return (
            pltpu.make_async_copy(
                feat_out.at[slot], out_ref.at[:, pl.ds(column, block)], sems.at[0, slot]
            ),
            pltpu.make_async_copy(
                cot_out.at[slot], out_ref.at[:, pl.ds(width + column, block)], sems.at[1, slot]
            ),
        )

    tenant_copy = pltpu.make_async_copy(
        tenant_rows, out_ref.at[:, pl.ds(2 * width, LANES)], tenant_sem
    )

    @pl.when(step == 0)
    def _():
        rows = lax.broadcasted_iota(jnp.int32, select.shape, 0)
        masks = [rows == slots for slots in route_slots(idx_ref[...], experts, capacity)]
        filled = sum(m.astype(jnp.float32) for m in masks)
        weight[...] = sum(
            jnp.sum(jnp.where(m, prob_ref[k : k + 1, :], 0.0), axis=1, keepdims=True)
            for k, m in enumerate(masks)
        )
        tenant = jnp.sum(filled * tenant_ref[...].astype(jnp.float32), axis=1, keepdims=True)
        tenant_rows[...] = jnp.broadcast_to(tenant, tenant_rows.shape).astype(jnp.bfloat16)
        tenant_copy.start()
        select[...] = filled.astype(jnp.bfloat16)

    @pl.when(step >= 2)
    def _():
        for copy in copies(step - 2, slot):
            copy.wait()

    feat_out[slot] = matmul(select[...], tok_ref[...]).astype(jnp.bfloat16)
    cot_out[slot] = (matmul(select[...], cot_ref[...]) * weight[...]).astype(jnp.bfloat16)
    for copy in copies(step, slot):
        copy.start()

    @pl.when(step == steps - 1)
    def _():
        for copy in copies(step - 1, 1 - slot):
            copy.wait()
        for copy in copies(step, slot):
            copy.wait()
        tenant_copy.wait()


def dispatch(idx, prob, tenant, tokens, cotangent, experts, capacity):
    tok_rows, width = tokens.shape
    rows = experts * capacity
    block = 2048
    return pl.pallas_call(
        functools.partial(dispatch_kernel, experts, capacity),
        out_shape=jax.ShapeDtypeStruct((rows, 2 * width + LANES), jnp.bfloat16),
        grid=(width // block,),
        in_specs=[
            pl.BlockSpec(idx.shape, lambda i: (0, 0)),
            pl.BlockSpec(prob.shape, lambda i: (0, 0)),
            pl.BlockSpec(tenant.shape, lambda i: (0, 0)),
            pl.BlockSpec((tok_rows, block), lambda i: (0, i)),
            pl.BlockSpec((tok_rows, block), lambda i: (0, i)),
        ],
        out_specs=pl.BlockSpec(memory_space=pl.ANY),
        scratch_shapes=[
            pltpu.VMEM((rows, tok_rows), jnp.bfloat16),
            pltpu.VMEM((rows, 1), jnp.float32),
            pltpu.VMEM((rows, LANES), jnp.bfloat16),
            pltpu.VMEM((2, rows, block), jnp.bfloat16),
            pltpu.VMEM((2, rows, block), jnp.bfloat16),
            pltpu.SemaphoreType.DMA((2, 2)),
            pltpu.SemaphoreType.DMA,
        ],
        compiler_params=pltpu.CompilerParams(vmem_limit_bytes=VMEM_BYTES),
        cost_estimate=pl.CostEstimate(
            flops=4 * rows * tok_rows * width,
            bytes_accessed=4 * tok_rows * width + 4 * rows * width,
            transcendentals=0,
        ),
        name="dispatch",
    )(idx, prob, tenant, tokens, cotangent)


def combine_kernel(experts, capacity, idx_ref, ret_ref, out_ref, select):
    @pl.when(pl.program_id(0) == 0)
    def _():
        slots = route_slots(idx_ref[...], experts, capacity)
        rows = lax.broadcasted_iota(jnp.int32, (8, slots[0].shape[1]), 0)
        table = sum(jnp.where(rows == k, s.astype(jnp.float32), 0.0) for k, s in enumerate(slots))
        table = table.T.astype(jnp.int32)
        lanes = lax.broadcasted_iota(jnp.int32, select.shape, 1)
        select[...] = sum(
            (lanes == table[:, k : k + 1]).astype(jnp.float32) for k in range(len(slots))
        ).astype(jnp.bfloat16)

    out_ref[...] = matmul(select[...], ret_ref[...]).astype(jnp.bfloat16)


def combine(idx, returned, experts, capacity):
    tok_rows, width = idx.shape[1], returned.shape[1]
    block = 2048
    rows = returned.shape[0]
    return pl.pallas_call(
        functools.partial(combine_kernel, experts, capacity),
        out_shape=jax.ShapeDtypeStruct((tok_rows, width), jnp.bfloat16),
        grid=(width // block,),
        in_specs=[
            pl.BlockSpec(idx.shape, lambda i: (0, 0)),
            pl.BlockSpec((rows, block), lambda i: (0, i)),
        ],
        out_specs=pl.BlockSpec((tok_rows, block), lambda i: (0, i)),
        scratch_shapes=[pltpu.VMEM((tok_rows, rows), jnp.bfloat16)],
        compiler_params=pltpu.CompilerParams(vmem_limit_bytes=VMEM_BYTES),
        cost_estimate=pl.CostEstimate(
            flops=2 * rows * tok_rows * width,
            bytes_accessed=2 * (rows + tok_rows) * width,
            transcendentals=0,
        ),
        name="combine",
    )(idx, returned)


def expert_kernel(
    rank,
    chips,
    got_ref,
    gate_ref,
    up_ref,
    down_ref,
    *refs,
):
    held_refs, route_out, part_outs = refs[:chips], refs[chips], refs[chips + 1 : 2 * chips + 1]
    expert_body(rank, got_ref, gate_ref, up_ref, down_ref, held_refs, route_out, part_outs, *refs[2 * chips + 1 :])


def expert_body(
    rank,
    got_ref,
    gate_ref,
    up_ref,
    down_ref,
    held_refs,
    route_out,
    part_outs,
    feat,
    cot,
    tenant,
    low_held,
    high_held,
    gate,
    up,
    down,
    grads,
    down_sum,
    up_sum,
    gate_pre,
    up_pre,
    low,
    low_t,
    back_t,
    high_gate,
    high_up,
    first_sems,
    sems,
    out_sems,
    route_sems,
):
    width = feat.shape[1]
    hidden = down.shape[0]
    groups, chip_rows = low_held.shape[0], held_refs[0].shape[0]
    block = 256
    step = 1024
    parts = hidden // block

    quarter = width // 4

    def first_copies(q):
        at = pl.ds(pl.multiple_of(q * quarter, quarter), quarter)
        return (
            pltpu.make_async_copy(got_ref.at[:, at], feat.at[:, at], first_sems.at[0, q]),
            pltpu.make_async_copy(gate_ref.at[at], gate.at[at], first_sems.at[1, q]),
        )

    later = [[], [], []]

    def plan(stage, source, target):
        number = sum(len(c) for c in later)
        later[stage].append(pltpu.make_async_copy(source, target, sems.at[number]))

    plan(0, got_ref.at[:, pl.ds(2 * width, LANES)], tenant)
    for c, held in enumerate(held_refs):
        rows = pl.ds(c * chip_rows, chip_rows)
        plan(0, held.at[:, pl.ds(0, width)], low_held.at[rows])
        plan(0, held.at[:, pl.ds(width, hidden)], high_held.at[rows])
    plan(1, up_ref, up)
    plan(2, got_ref.at[:, pl.ds(width, width)], cot)
    plan(2, down_ref, down)

    def begin(copies):
        for copy in copies:
            copy.start()

    def arrive(copies):
        for copy in copies:
            copy.wait()

    begin(first_copies(0))
    begin(first_copies(1))
    gate_pre[...] = jnp.zeros_like(gate_pre)

    def gate_step(q, carry):
        arrive(first_copies(q))
        pl.when(q < 2)(lambda: begin(first_copies(q + 2)))
        pl.when(q == 2)(lambda: begin(later[0]))
        pl.when(q == 3)(lambda: begin(later[1]))
        at = pl.ds(pl.multiple_of(q * quarter, quarter), quarter)
        for h in range(parts):
            to = slice(h * block, (h + 1) * block)
            gate_pre[:, to] += matmul(feat[:, at], gate[at, to])
        return carry

    lax.fori_loop(0, 4, gate_step, 0)
    arrive(later[0])
    begin(later[2])
    owner = lax.broadcasted_iota(jnp.int32, (1, groups), 1) // (2 * rank)
    selector = (tenant[:, 0:1].astype(jnp.int32) == owner).astype(jnp.float32)
    low[...] = (contract_last(feat[...], low_held[...]) * selector).astype(jnp.bfloat16)
    is_gate = lax.broadcasted_iota(jnp.int32, (groups, 1), 0) // rank % 2 == 0
    high = high_held[...].astype(jnp.float32)
    high_gate[...] = jnp.where(is_gate, high, 0.0).astype(jnp.bfloat16)
    high_up[...] = jnp.where(is_gate, 0.0, high).astype(jnp.bfloat16)
    arrive(later[1])

    def up_step(h, carry):
        at = pl.ds(pl.multiple_of(h * block, block), block)
        up_pre[:, at] = matmul(feat[...], up[:, at]) + adapter_scale * matmul(
            low[...], high_up[:, at]
        )
        return carry

    lax.fori_loop(0, parts, up_step, 0)
    arrive(later[2])

    def back_step(h, carry):
        at = pl.ds(pl.multiple_of(h * block, block), block)
        after = pl.ds(pl.multiple_of(hidden + h * block, block), block)
        back = contract_last(cot[...], down[at])
        pre = gate_pre[:, at] + adapter_scale * matmul(low[...], high_gate[:, at])
        sig = jax.nn.sigmoid(pre)
        grads[:, at] = (back * up_pre[:, at] * (sig + pre * sig * (1.0 - sig))).astype(jnp.bfloat16)
        grads[:, after] = (back * pre * sig).astype(jnp.bfloat16)
        return carry

    lax.fori_loop(0, parts, back_step, 0)
    low_back = contract_last(grads[:, :hidden], high_gate[...]) + contract_last(
        grads[:, hidden:], high_up[...]
    )
    low_back = (low_back * selector).astype(jnp.bfloat16)
    back_t[...] = low_back.astype(jnp.float32).T.astype(jnp.bfloat16)
    low_t[...] = low[...].astype(jnp.float32).T.astype(jnp.bfloat16)
    low[...] = low_back

    for h in range(parts):
        at = pl.ds(h * block, block)
        after = pl.ds(hidden + h * block, block)
        up_sum[:, at] = adapter_scale * jnp.where(
            is_gate, matmul(low_t[...], grads[:, at]), matmul(low_t[...], grads[:, after])
        )
    for i in range(width // step):
        at = pl.ds(i * step, step)
        down_sum[:, at] = adapter_scale * matmul(back_t[...], feat[:, at])
    leaving = []
    for c, part_out in enumerate(part_outs):
        rows = pl.ds(c * chip_rows, chip_rows)
        for source, at in ((up_sum, pl.ds(width, hidden)), (down_sum, pl.ds(0, width))):
            leaving.append(
                pltpu.make_async_copy(source.at[rows], part_out.at[:, at], out_sems.at[len(leaving)])
            )
    begin(leaving)

    def route_copy(i):
        at = pl.ds(i * step, step)
        return pltpu.make_async_copy(cot.at[:, at], route_out.at[:, at], route_sems.at[i])

    for i in range(width // step):
        at = pl.ds(i * step, step)
        cot[:, at] = (
            contract_last(grads[:, :hidden], gate[at])
            + contract_last(grads[:, hidden:], up[at])
            + adapter_scale * matmul(low[...], low_held[:, at])
        ).astype(jnp.bfloat16)
        route_copy(i).start()
    arrive(leaving)
    for i in range(width // step):
        route_copy(i).wait()


def expert_pass(received, gate_matrix, up_matrix, down_weight, held, rank):
    rows = received.shape[0]
    width, hidden = gate_matrix.shape
    chips, chip_rows = len(held), held[0].shape[0]
    groups = chips * chip_rows
    anywhere = pl.BlockSpec(memory_space=pl.ANY)
    return pl.pallas_call(
        functools.partial(expert_kernel, rank, chips),
        out_shape=(
            jax.ShapeDtypeStruct((rows, width), jnp.bfloat16),
            *[jax.ShapeDtypeStruct((chip_rows, width + hidden), jnp.float32)] * chips,
        ),
        in_specs=[anywhere] * (4 + chips),
        out_specs=(anywhere,) * (1 + chips),
        scratch_shapes=[
            pltpu.VMEM((rows, width), jnp.bfloat16),
            pltpu.VMEM((rows, width), jnp.bfloat16),
            pltpu.VMEM((rows, LANES), jnp.bfloat16),
            pltpu.VMEM((groups, width), jnp.bfloat16),
            pltpu.VMEM((groups, hidden), jnp.bfloat16),
            pltpu.VMEM((width, hidden), jnp.bfloat16),
            pltpu.VMEM((width, hidden), jnp.bfloat16),
            pltpu.VMEM((hidden, width), jnp.bfloat16),
            pltpu.VMEM((rows, 2 * hidden), jnp.bfloat16),
            pltpu.VMEM((groups, width), jnp.float32),
            pltpu.VMEM((groups, hidden), jnp.float32),
            pltpu.VMEM((rows, hidden), jnp.float32),
            pltpu.VMEM((rows, hidden), jnp.float32),
            pltpu.VMEM((rows, groups), jnp.bfloat16),
            pltpu.VMEM((groups, rows), jnp.bfloat16),
            pltpu.VMEM((groups, rows), jnp.bfloat16),
            pltpu.VMEM((groups, hidden), jnp.bfloat16),
            pltpu.VMEM((groups, hidden), jnp.bfloat16),
            pltpu.SemaphoreType.DMA((2, 4)),
            pltpu.SemaphoreType.DMA((4 + 2 * chips,)),
            pltpu.SemaphoreType.DMA((2 * chips,)),
            pltpu.SemaphoreType.DMA((width // 1024,)),
        ],
        compiler_params=pltpu.CompilerParams(vmem_limit_bytes=VMEM_BYTES),
        cost_estimate=pl.CostEstimate(
            flops=10 * rows * width * hidden + 6 * rows * width * groups,
            bytes_accessed=6 * width * hidden + 6 * rows * width,
            transcendentals=rows * hidden,
        ),
        name="expert_pass",
    )(received, gate_matrix, up_matrix, down_weight, *held)


def along_x(rows, step):
    devices = lax.axis_size("dp")
    return lax.ppermute(rows, "dp", [(i, (i + 2 * step) % devices) for i in range(devices)])


def other_core(rows):
    return lax.ppermute(rows, "dp", [(i, i ^ 1) for i in range(lax.axis_size("dp"))])


def exchange(named, rows):
    return lax.cond(
        named,
        lambda r: lax.all_to_all(r, "expert", split_axis=0, concat_axis=0, tiled=True),
        jnp.zeros_like,
        rows,
    )


def local(
    tokens,
    cotangent,
    routed_expert_index,
    router_gate_weights,
    token_tenant_index,
    frozen_gate_weight,
    frozen_up_weight,
    frozen_down_weight,
    adapter_down_matrices,
    adapter_up_matrices,
):
    experts = lax.axis_size("expert")
    tenants = lax.axis_size("dp")
    tok_rows, width = tokens.shape
    routes = routed_expert_index.shape[1]
    hidden = frozen_gate_weight.shape[2]
    rank = adapter_down_matrices.shape[3]
    capacity = 5 * tok_rows * routes // (4 * experts)
    idx = routed_expert_index.T
    prob = router_gate_weights.T
    me = lax.axis_index("dp")
    chips = tenants // 2
    tenant = (me // 2 - token_tenant_index // 2) % chips * 2 + (me + token_tenant_index) % 2
    tenant = tenant.reshape(1, tok_rows)
    adapters = jnp.concatenate([adapter_down_matrices[0, 0], adapter_up_matrices[0, 0]], axis=-1)
    adapters = adapters.reshape(2 * rank, width + hidden)
    named = me < tenants
    sent = dispatch(idx, prob, tenant, tokens, cotangent, experts, capacity)
    sent, others = lax.optimization_barrier((sent, other_core(adapters)))
    pair = jnp.concatenate([adapters, others], axis=0)
    held = [pair] + [along_x(pair, step) for step in range(1, chips)]
    received = exchange(named, sent)
    received, *held = lax.optimization_barrier((received, *held))
    route_grad, own, *parts = expert_pass(
        received,
        frozen_gate_weight[0],
        frozen_up_weight[0],
        frozen_down_weight[0],
        held,
        rank,
    )
    arrived = [along_x(part, -step) for step, part in enumerate(parts, 1)]
    returned = exchange(named, route_grad)
    returned, own, *arrived = lax.optimization_barrier((returned, own, *arrived))
    token_grads = combine(idx, returned, experts, capacity)
    total = sum(arrived, own)
    owned = total[: 2 * rank] + other_core(total[2 * rank :])
    down_owned = owned[:, :width].reshape(1, 1, 2, rank, width)
    up_owned = owned[:, width:].reshape(1, 1, 2, rank, hidden)
    return token_grads, down_owned, up_owned


def solution(mesh):
    in_specs = (
        P(("dp", "expert"), None),
        P(("dp", "expert"), None),
        P(("dp", "expert"), None),
        P(("dp", "expert"), None),
        P(("dp", "expert")),
        P("expert", None, None),
        P("expert", None, None),
        P("expert", None, None),
        P("dp", "expert", None, None, None),
        P("dp", "expert", None, None, None),
    )
    out_specs = (
        P(("dp", "expert"), None),
        P("dp", "expert", None, None, None),
        P("dp", "expert", None, None, None),
    )
    return jax.shard_map(local, mesh=mesh, in_specs=in_specs, out_specs=out_specs, check_vma=False)
```

```python
import functools

import jax
import jax.numpy as jnp
from jax import lax
from jax.experimental import pallas as pl
from jax.experimental.pallas import tpu as pltpu
from jax.sharding import PartitionSpec as P

adapter_scale = 0.5
LANES = 128
VMEM_BYTES = 60 * 1024 * 1024
EXPERT_VMEM_BYTES = 48 * 1024 * 1024


def contract_last(left_side, right_side):
    return lax.dot_general(
        left_side, right_side, (((1,), (1,)), ((), ())), preferred_element_type=jnp.float32
    )


def matmul(left_side, right_side):
    return jnp.dot(left_side, right_side, preferred_element_type=jnp.float32)


def route_slots(idx, experts, capacity):
    routes, tok_rows = idx.shape
    names = lax.broadcasted_iota(jnp.int32, (experts, tok_rows), 0)
    members = [(idx[k : k + 1, :] == names).astype(jnp.float32) for k in range(routes)]
    before = (
        lax.broadcasted_iota(jnp.int32, (tok_rows, tok_rows), 0)
        < lax.broadcasted_iota(jnp.int32, (tok_rows, tok_rows), 1)
    ).astype(jnp.bfloat16)
    running = matmul(sum(members).astype(jnp.bfloat16), before)
    return [
        idx[k : k + 1, :] * capacity
        + jnp.sum(running * member, axis=0, keepdims=True).astype(jnp.int32)
        for k, member in enumerate(members)
    ]


def dispatch_kernel(
    experts,
    capacity,
    chips,
    me_ref,
    idx_ref,
    prob_ref,
    tenant_ref,
    tok_ref,
    cot_ref,
    out_ref,
    select,
    weight,
    tenant_rows,
    feat_out,
    cot_out,
    sems,
    tenant_sem,
):
    step = pl.program_id(0)
    steps = pl.num_programs(0)
    block = tok_ref.shape[1]
    width = block * steps
    slot = lax.rem(step, 2)

    def copies(at, slot):
        column = pl.multiple_of(at * block, block)
        return (
            pltpu.make_async_copy(
                feat_out.at[slot], out_ref.at[:, pl.ds(column, block)], sems.at[0, slot]
            ),
            pltpu.make_async_copy(
                cot_out.at[slot], out_ref.at[:, pl.ds(width + column, block)], sems.at[1, slot]
            ),
        )

    tenant_copy = pltpu.make_async_copy(
        tenant_rows, out_ref.at[:, pl.ds(2 * width, LANES)], tenant_sem
    )

    @pl.when(step == 0)
    def _():
        rows = lax.broadcasted_iota(jnp.int32, select.shape, 0)
        masks = [rows == slots for slots in route_slots(idx_ref[...], experts, capacity)]
        filled = sum(m.astype(jnp.float32) for m in masks)
        weight[...] = sum(
            jnp.sum(jnp.where(m, prob_ref[k : k + 1, :], 0.0), axis=1, keepdims=True)
            for k, m in enumerate(masks)
        )
        me, owner = me_ref[0], tenant_ref[...]
        place = lax.rem(me // 2 + chips - lax.div(owner, 2), chips) * 2 + lax.rem(me + owner, 2)
        tenant = jnp.sum(filled * place.astype(jnp.float32), axis=1, keepdims=True)
        tenant_rows[...] = jnp.broadcast_to(tenant, tenant_rows.shape).astype(jnp.bfloat16)
        tenant_copy.start()
        select[...] = filled.astype(jnp.bfloat16)

    @pl.when(step >= 2)
    def _():
        for copy in copies(step - 2, slot):
            copy.wait()

    feat_out[slot] = matmul(select[...], tok_ref[...]).astype(jnp.bfloat16)
    cot_out[slot] = (matmul(select[...], cot_ref[...]) * weight[...]).astype(jnp.bfloat16)
    for copy in copies(step, slot):
        copy.start()

    @pl.when(step == steps - 1)
    def _():
        for copy in copies(step - 1, 1 - slot):
            copy.wait()
        for copy in copies(step, slot):
            copy.wait()
        tenant_copy.wait()


def dispatch(me, idx, prob, tenant, tokens, cotangent, experts, capacity, chips):
    tok_rows, width = tokens.shape
    rows = experts * capacity
    block = 2048
    return pl.pallas_call(
        functools.partial(dispatch_kernel, experts, capacity, chips),
        out_shape=jax.ShapeDtypeStruct((rows, 2 * width + LANES), jnp.bfloat16),
        grid=(width // block,),
        in_specs=[
            pl.BlockSpec(memory_space=pltpu.SMEM),
            pl.BlockSpec(idx.shape, lambda i: (0, 0)),
            pl.BlockSpec(prob.shape, lambda i: (0, 0)),
            pl.BlockSpec(tenant.shape, lambda i: (0, 0)),
            pl.BlockSpec((tok_rows, block), lambda i: (0, i)),
            pl.BlockSpec((tok_rows, block), lambda i: (0, i)),
        ],
        out_specs=pl.BlockSpec(memory_space=pl.ANY),
        scratch_shapes=[
            pltpu.VMEM((rows, tok_rows), jnp.bfloat16),
            pltpu.VMEM((rows, 1), jnp.float32),
            pltpu.VMEM((rows, LANES), jnp.bfloat16),
            pltpu.VMEM((2, rows, block), jnp.bfloat16),
            pltpu.VMEM((2, rows, block), jnp.bfloat16),
            pltpu.SemaphoreType.DMA((2, 2)),
            pltpu.SemaphoreType.DMA,
        ],
        compiler_params=pltpu.CompilerParams(vmem_limit_bytes=VMEM_BYTES),
        cost_estimate=pl.CostEstimate(
            flops=4 * rows * tok_rows * width,
            bytes_accessed=4 * tok_rows * width + 4 * rows * width,
            transcendentals=0,
        ),
        name="dispatch",
    )(me.reshape(1), idx, prob, tenant, tokens, cotangent)


def combine_kernel(experts, capacity, idx_ref, ret_ref, out_ref, select):
    @pl.when(pl.program_id(0) == 0)
    def _():
        slots = route_slots(idx_ref[...], experts, capacity)
        rows = lax.broadcasted_iota(jnp.int32, (8, slots[0].shape[1]), 0)
        table = sum(jnp.where(rows == k, s.astype(jnp.float32), 0.0) for k, s in enumerate(slots))
        table = table.T.astype(jnp.int32)
        lanes = lax.broadcasted_iota(jnp.int32, select.shape, 1)
        select[...] = sum(
            (lanes == table[:, k : k + 1]).astype(jnp.float32) for k in range(len(slots))
        ).astype(jnp.bfloat16)

    out_ref[...] = matmul(select[...], ret_ref[...]).astype(jnp.bfloat16)


def combine(idx, returned, experts, capacity):
    tok_rows, width = idx.shape[1], returned.shape[1]
    block = 2048
    rows = returned.shape[0]
    return pl.pallas_call(
        functools.partial(combine_kernel, experts, capacity),
        out_shape=jax.ShapeDtypeStruct((tok_rows, width), jnp.bfloat16),
        grid=(width // block,),
        in_specs=[
            pl.BlockSpec(idx.shape, lambda i: (0, 0)),
            pl.BlockSpec((rows, block), lambda i: (0, i)),
        ],
        out_specs=pl.BlockSpec((tok_rows, block), lambda i: (0, i)),
        scratch_shapes=[pltpu.VMEM((tok_rows, rows), jnp.bfloat16)],
        compiler_params=pltpu.CompilerParams(vmem_limit_bytes=VMEM_BYTES),
        cost_estimate=pl.CostEstimate(
            flops=2 * rows * tok_rows * width,
            bytes_accessed=2 * (rows + tok_rows) * width,
            transcendentals=0,
        ),
        name="combine",
    )(idx, returned)


def expert_kernel(
    rank,
    chips,
    got_ref,
    gate_ref,
    up_ref,
    down_ref,
    *refs,
):
    held_refs, route_out, part_outs = refs[:chips], refs[chips], refs[chips + 1 : 2 * chips + 1]
    expert_body(rank, got_ref, gate_ref, up_ref, down_ref, held_refs, route_out, part_outs, *refs[2 * chips + 1 :])


def expert_body(
    rank,
    got_ref,
    gate_ref,
    up_ref,
    down_ref,
    held_refs,
    route_out,
    part_outs,
    feat,
    cot,
    tenant,
    low_held,
    high_held,
    gate,
    up,
    down,
    grads,
    down_sum,
    up_sum,
    gate_pre,
    up_pre,
    low,
    low_t,
    back_t,
    high_gate,
    high_up,
    first_sems,
    sems,
    out_sems,
    route_sems,
):
    width = feat.shape[1]
    hidden = down.shape[0]
    groups, chip_rows = low_held.shape[0], held_refs[0].shape[0]
    block = 256
    step = 1024
    parts = hidden // block

    quarter = width // 4

    def first_copies(q):
        at = pl.ds(pl.multiple_of(q * quarter, quarter), quarter)
        return (
            pltpu.make_async_copy(got_ref.at[:, at], feat.at[:, at], first_sems.at[0, q]),
            pltpu.make_async_copy(gate_ref.at[at], gate.at[at], first_sems.at[1, q]),
        )

    later = [[], [], []]

    def plan(stage, source, target):
        number = sum(len(c) for c in later)
        later[stage].append(pltpu.make_async_copy(source, target, sems.at[number]))

    plan(0, got_ref.at[:, pl.ds(2 * width, LANES)], tenant)
    for c, held in enumerate(held_refs):
        rows = pl.ds(c * chip_rows, chip_rows)
        plan(0, held.at[:, pl.ds(0, width)], low_held.at[rows])
        plan(0, held.at[:, pl.ds(width, hidden)], high_held.at[rows])
    plan(1, up_ref, up)
    plan(2, got_ref.at[:, pl.ds(width, width)], cot)
    plan(2, down_ref, down)

    def begin(copies):
        for copy in copies:
            copy.start()

    def arrive(copies):
        for copy in copies:
            copy.wait()

    begin(first_copies(0))
    begin(first_copies(1))
    gate_pre[...] = jnp.zeros_like(gate_pre)

    def gate_step(q, carry):
        arrive(first_copies(q))
        pl.when(q < 2)(lambda: begin(first_copies(q + 2)))
        pl.when(q == 2)(lambda: begin(later[0]))
        pl.when(q == 3)(lambda: begin(later[1]))
        at = pl.ds(pl.multiple_of(q * quarter, quarter), quarter)
        for h in range(parts):
            to = slice(h * block, (h + 1) * block)
            gate_pre[:, to] += matmul(feat[:, at], gate[at, to])
        return carry

    lax.fori_loop(0, 4, gate_step, 0)
    arrive(later[0])
    begin(later[2])
    owner = lax.broadcasted_iota(jnp.int32, (1, groups), 1) // (2 * rank)
    selector = (tenant[:, 0:1].astype(jnp.int32) == owner).astype(jnp.float32)
    low[...] = (contract_last(feat[...], low_held[...]) * selector).astype(jnp.bfloat16)
    is_gate = lax.broadcasted_iota(jnp.int32, (groups, 1), 0) // rank % 2 == 0
    high = high_held[...].astype(jnp.float32)
    high_gate[...] = jnp.where(is_gate, high, 0.0).astype(jnp.bfloat16)
    high_up[...] = jnp.where(is_gate, 0.0, high).astype(jnp.bfloat16)
    arrive(later[1])

    def up_step(h, carry):
        at = pl.ds(pl.multiple_of(h * block, block), block)
        up_pre[:, at] = matmul(feat[...], up[:, at]) + adapter_scale * matmul(
            low[...], high_up[:, at]
        )
        return carry

    lax.fori_loop(0, parts, up_step, 0)
    arrive(later[2])

    def back_step(h, carry):
        at = pl.ds(pl.multiple_of(h * block, block), block)
        after = pl.ds(pl.multiple_of(hidden + h * block, block), block)
        back = contract_last(cot[...], down[at])
        pre = gate_pre[:, at] + adapter_scale * matmul(low[...], high_gate[:, at])
        sig = jax.nn.sigmoid(pre)
        grads[:, at] = (back * up_pre[:, at] * (sig + pre * sig * (1.0 - sig))).astype(jnp.bfloat16)
        grads[:, after] = (back * pre * sig).astype(jnp.bfloat16)
        return carry

    lax.fori_loop(0, parts, back_step, 0)
    low_back = contract_last(grads[:, :hidden], high_gate[...]) + contract_last(
        grads[:, hidden:], high_up[...]
    )
    low_back = (low_back * selector).astype(jnp.bfloat16)
    back_t[...] = low_back.astype(jnp.float32).T.astype(jnp.bfloat16)
    low_t[...] = low[...].astype(jnp.float32).T.astype(jnp.bfloat16)
    low[...] = low_back

    for h in range(parts):
        at = pl.ds(h * block, block)
        after = pl.ds(hidden + h * block, block)
        up_sum[:, at] = adapter_scale * jnp.where(
            is_gate, matmul(low_t[...], grads[:, at]), matmul(low_t[...], grads[:, after])
        )
    for i in range(width // step):
        at = pl.ds(i * step, step)
        down_sum[:, at] = adapter_scale * matmul(back_t[...], feat[:, at])
    leaving = []
    for c, part_out in enumerate(part_outs):
        rows = pl.ds(c * chip_rows, chip_rows)
        for source, at in ((up_sum, pl.ds(width, hidden)), (down_sum, pl.ds(0, width))):
            leaving.append(
                pltpu.make_async_copy(source.at[rows], part_out.at[:, at], out_sems.at[len(leaving)])
            )
    begin(leaving)

    def route_copy(i):
        at = pl.ds(i * step, step)
        return pltpu.make_async_copy(cot.at[:, at], route_out.at[:, at], route_sems.at[i])

    for i in range(width // step):
        at = pl.ds(i * step, step)
        cot[:, at] = (
            contract_last(grads[:, :hidden], gate[at])
            + contract_last(grads[:, hidden:], up[at])
            + adapter_scale * matmul(low[...], low_held[:, at])
        ).astype(jnp.bfloat16)
        route_copy(i).start()
    arrive(leaving)
    for i in range(width // step):
        route_copy(i).wait()


def expert_pass(received, gate_matrix, up_matrix, down_weight, held, rank):
    rows = received.shape[0]
    width, hidden = gate_matrix.shape
    chips, chip_rows = len(held), held[0].shape[0]
    groups = chips * chip_rows
    anywhere = pl.BlockSpec(memory_space=pl.ANY)
    return pl.pallas_call(
        functools.partial(expert_kernel, rank, chips),
        out_shape=(
            jax.ShapeDtypeStruct((rows, width), jnp.bfloat16),
            *[jax.ShapeDtypeStruct((chip_rows, width + hidden), jnp.float32)] * chips,
        ),
        in_specs=[anywhere] * (4 + chips),
        out_specs=(anywhere,) * (1 + chips),
        scratch_shapes=[
            pltpu.VMEM((rows, width), jnp.bfloat16),
            pltpu.VMEM((rows, width), jnp.bfloat16),
            pltpu.VMEM((rows, LANES), jnp.bfloat16),
            pltpu.VMEM((groups, width), jnp.bfloat16),
            pltpu.VMEM((groups, hidden), jnp.bfloat16),
            pltpu.VMEM((width, hidden), jnp.bfloat16),
            pltpu.VMEM((width, hidden), jnp.bfloat16),
            pltpu.VMEM((hidden, width), jnp.bfloat16),
            pltpu.VMEM((rows, 2 * hidden), jnp.bfloat16),
            pltpu.VMEM((groups, width), jnp.float32),
            pltpu.VMEM((groups, hidden), jnp.float32),
            pltpu.VMEM((rows, hidden), jnp.float32),
            pltpu.VMEM((rows, hidden), jnp.float32),
            pltpu.VMEM((rows, groups), jnp.bfloat16),
            pltpu.VMEM((groups, rows), jnp.bfloat16),
            pltpu.VMEM((groups, rows), jnp.bfloat16),
            pltpu.VMEM((groups, hidden), jnp.bfloat16),
            pltpu.VMEM((groups, hidden), jnp.bfloat16),
            pltpu.SemaphoreType.DMA((2, 4)),
            pltpu.SemaphoreType.DMA((4 + 2 * chips,)),
            pltpu.SemaphoreType.DMA((2 * chips,)),
            pltpu.SemaphoreType.DMA((width // 1024,)),
        ],
        compiler_params=pltpu.CompilerParams(vmem_limit_bytes=EXPERT_VMEM_BYTES),
        cost_estimate=pl.CostEstimate(
            flops=10 * rows * width * hidden + 6 * rows * width * groups,
            bytes_accessed=6 * width * hidden + 6 * rows * width,
            transcendentals=rows * hidden,
        ),
        name="expert_pass",
    )(received, gate_matrix, up_matrix, down_weight, *held)


def along_x(rows, step):
    devices = lax.axis_size("dp")
    return lax.ppermute(rows, "dp", [(i, (i + 2 * step) % devices) for i in range(devices)])


def other_core(rows):
    return lax.ppermute(rows, "dp", [(i, i ^ 1) for i in range(lax.axis_size("dp"))])


def exchange(named, rows):
    return lax.cond(
        named,
        lambda r: lax.all_to_all(r, "expert", split_axis=0, concat_axis=0, tiled=True),
        jnp.zeros_like,
        rows,
    )


def local(
    tokens,
    cotangent,
    routed_expert_index,
    router_gate_weights,
    token_tenant_index,
    frozen_gate_weight,
    frozen_up_weight,
    frozen_down_weight,
    adapter_down_matrices,
    adapter_up_matrices,
):
    experts = lax.axis_size("expert")
    tenants = lax.axis_size("dp")
    tok_rows, width = tokens.shape
    routes = routed_expert_index.shape[1]
    hidden = frozen_gate_weight.shape[2]
    rank = adapter_down_matrices.shape[3]
    capacity = 5 * tok_rows * routes // (4 * experts)
    idx = routed_expert_index.T
    prob = router_gate_weights.T
    me = lax.axis_index("dp")
    chips = tenants // 2
    tenant = token_tenant_index.reshape(1, tok_rows)
    adapters = jnp.concatenate([adapter_down_matrices[0, 0], adapter_up_matrices[0, 0]], axis=-1)
    adapters = adapters.reshape(2 * rank, width + hidden)
    named = me < tenants
    sent = dispatch(me, idx, prob, tenant, tokens, cotangent, experts, capacity, chips)
    sent, others = lax.optimization_barrier((sent, other_core(adapters)))
    pair = jnp.concatenate([adapters, others], axis=0)
    held = [pair] + [along_x(pair, step) for step in range(1, chips)]
    received = exchange(named, sent)
    received, *held = lax.optimization_barrier((received, *held))
    route_grad, own, *parts = expert_pass(
        received,
        frozen_gate_weight[0],
        frozen_up_weight[0],
        frozen_down_weight[0],
        held,
        rank,
    )
    arrived = [along_x(part, -step) for step, part in enumerate(parts, 1)]
    returned = exchange(named, route_grad)
    returned, own, *arrived = lax.optimization_barrier((returned, own, *arrived))
    token_grads = combine(idx, returned, experts, capacity)
    total = sum(arrived, own)
    owned = total[: 2 * rank] + other_core(total[2 * rank :])
    down_owned = owned[:, :width].reshape(1, 1, 2, rank, width)
    up_owned = owned[:, width:].reshape(1, 1, 2, rank, hidden)
    return token_grads, down_owned, up_owned


def solution(mesh):
    in_specs = (
        P(("dp", "expert"), None),
        P(("dp", "expert"), None),
        P(("dp", "expert"), None),
        P(("dp", "expert"), None),
        P(("dp", "expert")),
        P("expert", None, None),
        P("expert", None, None),
        P("expert", None, None),
        P("dp", "expert", None, None, None),
        P("dp", "expert", None, None, None),
    )
    out_specs = (
        P(("dp", "expert"), None),
        P("dp", "expert", None, None, None),
        P("dp", "expert", None, None, None),
    )
    return jax.shard_map(local, mesh=mesh, in_specs=in_specs, out_specs=out_specs, check_vma=False)
```

```python
import functools

import jax
import jax.numpy as jnp
from jax import lax
from jax.experimental import pallas as pl
from jax.experimental.pallas import tpu as pltpu
from jax.sharding import PartitionSpec as P

adapter_scale = 0.5
LANES = 128
VMEM_BYTES = 60 * 1024 * 1024
EXPERT_VMEM_BYTES = 52 * 1024 * 1024


def contract_last(left_side, right_side):
    return lax.dot_general(
        left_side, right_side, (((1,), (1,)), ((), ())), preferred_element_type=jnp.float32
    )


def matmul(left_side, right_side):
    return jnp.dot(left_side, right_side, preferred_element_type=jnp.float32)


def route_slots(idx, experts, capacity):
    routes, tok_rows = idx.shape
    names = lax.broadcasted_iota(jnp.int32, (experts, tok_rows), 0)
    members = [(idx[k : k + 1, :] == names).astype(jnp.float32) for k in range(routes)]
    before = (
        lax.broadcasted_iota(jnp.int32, (tok_rows, tok_rows), 0)
        < lax.broadcasted_iota(jnp.int32, (tok_rows, tok_rows), 1)
    ).astype(jnp.bfloat16)
    running = matmul(sum(members).astype(jnp.bfloat16), before)
    return [
        idx[k : k + 1, :] * capacity
        + jnp.sum(running * member, axis=0, keepdims=True).astype(jnp.int32)
        for k, member in enumerate(members)
    ]


def dispatch_kernel(
    experts,
    capacity,
    chips,
    me_ref,
    idx_ref,
    prob_ref,
    tenant_ref,
    tok_ref,
    cot_ref,
    out_ref,
    select,
    weight,
    tenant_rows,
    feat_out,
    cot_out,
    sems,
    tenant_sem,
):
    step = pl.program_id(0)
    steps = pl.num_programs(0)
    block = tok_ref.shape[1]
    width = block * steps
    slot = lax.rem(step, 2)

    def copies(at, slot):
        column = pl.multiple_of(at * block, block)
        return (
            pltpu.make_async_copy(
                feat_out.at[slot], out_ref.at[:, pl.ds(column, block)], sems.at[0, slot]
            ),
            pltpu.make_async_copy(
                cot_out.at[slot], out_ref.at[:, pl.ds(width + column, block)], sems.at[1, slot]
            ),
        )

    tenant_copy = pltpu.make_async_copy(
        tenant_rows, out_ref.at[:, pl.ds(2 * width, LANES)], tenant_sem
    )

    @pl.when(step == 0)
    def _():
        rows = lax.broadcasted_iota(jnp.int32, select.shape, 0)
        masks = [rows == slots for slots in route_slots(idx_ref[...], experts, capacity)]
        filled = sum(m.astype(jnp.float32) for m in masks)
        weight[...] = sum(
            jnp.sum(jnp.where(m, prob_ref[k : k + 1, :], 0.0), axis=1, keepdims=True)
            for k, m in enumerate(masks)
        )
        me, owner = me_ref[0], tenant_ref[...]
        place = lax.rem(me // 2 + chips - lax.div(owner, 2), chips) * 2 + lax.rem(me + owner, 2)
        tenant = jnp.sum(filled * place.astype(jnp.float32), axis=1, keepdims=True)
        tenant_rows[...] = jnp.broadcast_to(tenant, tenant_rows.shape).astype(jnp.bfloat16)
        tenant_copy.start()
        select[...] = filled.astype(jnp.bfloat16)

    @pl.when(step >= 2)
    def _():
        for copy in copies(step - 2, slot):
            copy.wait()

    feat_out[slot] = matmul(select[...], tok_ref[...]).astype(jnp.bfloat16)
    cot_out[slot] = (matmul(select[...], cot_ref[...]) * weight[...]).astype(jnp.bfloat16)
    for copy in copies(step, slot):
        copy.start()

    @pl.when(step == steps - 1)
    def _():
        for copy in copies(step - 1, 1 - slot):
            copy.wait()
        for copy in copies(step, slot):
            copy.wait()
        tenant_copy.wait()


def dispatch(me, idx, prob, tenant, tokens, cotangent, experts, capacity, chips):
    tok_rows, width = tokens.shape
    rows = experts * capacity
    block = 2048
    return pl.pallas_call(
        functools.partial(dispatch_kernel, experts, capacity, chips),
        out_shape=jax.ShapeDtypeStruct((rows, 2 * width + LANES), jnp.bfloat16),
        grid=(width // block,),
        in_specs=[
            pl.BlockSpec(memory_space=pltpu.SMEM),
            pl.BlockSpec(idx.shape, lambda i: (0, 0)),
            pl.BlockSpec(prob.shape, lambda i: (0, 0)),
            pl.BlockSpec(tenant.shape, lambda i: (0, 0)),
            pl.BlockSpec((tok_rows, block), lambda i: (0, i)),
            pl.BlockSpec((tok_rows, block), lambda i: (0, i)),
        ],
        out_specs=pl.BlockSpec(memory_space=pl.ANY),
        scratch_shapes=[
            pltpu.VMEM((rows, tok_rows), jnp.bfloat16),
            pltpu.VMEM((rows, 1), jnp.float32),
            pltpu.VMEM((rows, LANES), jnp.bfloat16),
            pltpu.VMEM((2, rows, block), jnp.bfloat16),
            pltpu.VMEM((2, rows, block), jnp.bfloat16),
            pltpu.SemaphoreType.DMA((2, 2)),
            pltpu.SemaphoreType.DMA,
        ],
        compiler_params=pltpu.CompilerParams(vmem_limit_bytes=VMEM_BYTES),
        cost_estimate=pl.CostEstimate(
            flops=4 * rows * tok_rows * width,
            bytes_accessed=4 * tok_rows * width + 4 * rows * width,
            transcendentals=0,
        ),
        name="dispatch",
    )(me.reshape(1), idx, prob, tenant, tokens, cotangent)


def combine_kernel(experts, capacity, idx_ref, ret_ref, out_ref, select):
    @pl.when(pl.program_id(0) == 0)
    def _():
        slots = route_slots(idx_ref[...], experts, capacity)
        rows = lax.broadcasted_iota(jnp.int32, (8, slots[0].shape[1]), 0)
        table = sum(jnp.where(rows == k, s.astype(jnp.float32), 0.0) for k, s in enumerate(slots))
        table = table.T.astype(jnp.int32)
        lanes = lax.broadcasted_iota(jnp.int32, select.shape, 1)
        select[...] = sum(
            (lanes == table[:, k : k + 1]).astype(jnp.float32) for k in range(len(slots))
        ).astype(jnp.bfloat16)

    out_ref[...] = matmul(select[...], ret_ref[...]).astype(jnp.bfloat16)


def combine(idx, returned, experts, capacity):
    tok_rows, width = idx.shape[1], returned.shape[1]
    block = 2048
    rows = returned.shape[0]
    return pl.pallas_call(
        functools.partial(combine_kernel, experts, capacity),
        out_shape=jax.ShapeDtypeStruct((tok_rows, width), jnp.bfloat16),
        grid=(width // block,),
        in_specs=[
            pl.BlockSpec(idx.shape, lambda i: (0, 0)),
            pl.BlockSpec((rows, block), lambda i: (0, i)),
        ],
        out_specs=pl.BlockSpec((tok_rows, block), lambda i: (0, i)),
        scratch_shapes=[pltpu.VMEM((tok_rows, rows), jnp.bfloat16)],
        compiler_params=pltpu.CompilerParams(vmem_limit_bytes=VMEM_BYTES),
        cost_estimate=pl.CostEstimate(
            flops=2 * rows * tok_rows * width,
            bytes_accessed=2 * (rows + tok_rows) * width,
            transcendentals=0,
        ),
        name="combine",
    )(idx, returned)


def expert_kernel(
    rank,
    chips,
    got_ref,
    gate_ref,
    up_ref,
    down_ref,
    *refs,
):
    held_refs, route_out, part_outs = refs[:chips], refs[chips], refs[chips + 1 : 2 * chips + 1]
    expert_body(rank, got_ref, gate_ref, up_ref, down_ref, held_refs, route_out, part_outs, *refs[2 * chips + 1 :])


def expert_body(
    rank,
    got_ref,
    gate_ref,
    up_ref,
    down_ref,
    held_refs,
    route_out,
    part_outs,
    feat,
    cot,
    tenant,
    low_held,
    high_held,
    gate,
    up,
    down,
    grads,
    down_sum,
    up_sum,
    gate_pre,
    up_pre,
    low,
    low_t,
    back_t,
    high_gate,
    high_up,
    first_sems,
    sems,
    out_sems,
    route_sems,
):
    width = feat.shape[1]
    hidden = down.shape[0]
    groups, chip_rows = low_held.shape[0], held_refs[0].shape[0]
    block = 256
    step = 1024
    parts = hidden // block

    quarter = width // 4

    def first_copies(q):
        at = pl.ds(pl.multiple_of(q * quarter, quarter), quarter)
        return (
            pltpu.make_async_copy(got_ref.at[:, at], feat.at[:, at], first_sems.at[0, q]),
            pltpu.make_async_copy(gate_ref.at[at], gate.at[at], first_sems.at[1, q]),
        )

    later = [[], [], []]

    def plan(stage, source, target):
        number = sum(len(c) for c in later)
        later[stage].append(pltpu.make_async_copy(source, target, sems.at[number]))

    plan(0, got_ref.at[:, pl.ds(2 * width, LANES)], tenant)
    for c, held in enumerate(held_refs):
        rows = pl.ds(c * chip_rows, chip_rows)
        plan(0, held.at[:, pl.ds(0, width)], low_held.at[rows])
        plan(0, held.at[:, pl.ds(width, hidden)], high_held.at[rows])
    plan(1, up_ref, up)
    plan(2, got_ref.at[:, pl.ds(width, width)], cot)
    plan(2, down_ref, down)

    def begin(copies):
        for copy in copies:
            copy.start()

    def arrive(copies):
        for copy in copies:
            copy.wait()

    begin(first_copies(0))
    begin(first_copies(1))
    gate_pre[...] = jnp.zeros_like(gate_pre)

    def gate_step(q, carry):
        arrive(first_copies(q))
        pl.when(q < 2)(lambda: begin(first_copies(q + 2)))
        pl.when(q == 2)(lambda: begin(later[0]))
        pl.when(q == 3)(lambda: begin(later[1]))
        at = pl.ds(pl.multiple_of(q * quarter, quarter), quarter)
        for h in range(parts):
            to = slice(h * block, (h + 1) * block)
            gate_pre[:, to] += matmul(feat[:, at], gate[at, to])
        return carry

    lax.fori_loop(0, 4, gate_step, 0)
    arrive(later[0])
    begin(later[2])
    owner = lax.broadcasted_iota(jnp.int32, (1, groups), 1) // (2 * rank)
    selector = (tenant[:, 0:1].astype(jnp.int32) == owner).astype(jnp.float32)
    low[...] = (contract_last(feat[...], low_held[...]) * selector).astype(jnp.bfloat16)
    is_gate = lax.broadcasted_iota(jnp.int32, (groups, 1), 0) // rank % 2 == 0
    high = high_held[...].astype(jnp.float32)
    high_gate[...] = jnp.where(is_gate, high, 0.0).astype(jnp.bfloat16)
    high_up[...] = jnp.where(is_gate, 0.0, high).astype(jnp.bfloat16)
    arrive(later[1])

    def up_step(h, carry):
        at = pl.ds(pl.multiple_of(h * block, block), block)
        up_pre[:, at] = matmul(feat[...], up[:, at]) + adapter_scale * matmul(
            low[...], high_up[:, at]
        )
        return carry

    lax.fori_loop(0, parts, up_step, 0)
    arrive(later[2])

    def back_step(h, carry):
        at = pl.ds(pl.multiple_of(h * block, block), block)
        after = pl.ds(pl.multiple_of(hidden + h * block, block), block)
        back = contract_last(cot[...], down[at])
        pre = gate_pre[:, at] + adapter_scale * matmul(low[...], high_gate[:, at])
        sig = jax.nn.sigmoid(pre)
        grads[:, at] = (back * up_pre[:, at] * (sig + pre * sig * (1.0 - sig))).astype(jnp.bfloat16)
        grads[:, after] = (back * pre * sig).astype(jnp.bfloat16)
        return carry

    lax.fori_loop(0, parts, back_step, 0)
    low_back = contract_last(grads[:, :hidden], high_gate[...]) + contract_last(
        grads[:, hidden:], high_up[...]
    )
    low_back = (low_back * selector).astype(jnp.bfloat16)
    back_t[...] = low_back.astype(jnp.float32).T.astype(jnp.bfloat16)
    low_t[...] = low[...].astype(jnp.float32).T.astype(jnp.bfloat16)
    low[...] = low_back

    for h in range(parts):
        at = pl.ds(h * block, block)
        after = pl.ds(hidden + h * block, block)
        up_sum[:, at] = adapter_scale * jnp.where(
            is_gate, matmul(low_t[...], grads[:, at]), matmul(low_t[...], grads[:, after])
        )
    for i in range(width // step):
        at = pl.ds(i * step, step)
        down_sum[:, at] = adapter_scale * matmul(back_t[...], feat[:, at])
    leaving = []
    for c, part_out in enumerate(part_outs):
        rows = pl.ds(c * chip_rows, chip_rows)
        for source, at in ((up_sum, pl.ds(width, hidden)), (down_sum, pl.ds(0, width))):
            leaving.append(
                pltpu.make_async_copy(source.at[rows], part_out.at[:, at], out_sems.at[len(leaving)])
            )
    begin(leaving)

    def route_copy(i):
        at = pl.ds(i * step, step)
        return pltpu.make_async_copy(cot.at[:, at], route_out.at[:, at], route_sems.at[i])

    for i in range(width // step):
        at = pl.ds(i * step, step)
        cot[:, at] = (
            contract_last(grads[:, :hidden], gate[at])
            + contract_last(grads[:, hidden:], up[at])
            + adapter_scale * matmul(low[...], low_held[:, at])
        ).astype(jnp.bfloat16)
        route_copy(i).start()
    arrive(leaving)
    for i in range(width // step):
        route_copy(i).wait()


def expert_pass(received, gate_matrix, up_matrix, down_weight, held, rank):
    rows = received.shape[0]
    width, hidden = gate_matrix.shape
    chips, chip_rows = len(held), held[0].shape[0]
    groups = chips * chip_rows
    anywhere = pl.BlockSpec(memory_space=pl.ANY)
    return pl.pallas_call(
        functools.partial(expert_kernel, rank, chips),
        out_shape=(
            jax.ShapeDtypeStruct((rows, width), jnp.bfloat16),
            *[jax.ShapeDtypeStruct((chip_rows, width + hidden), jnp.float32)] * chips,
        ),
        in_specs=[anywhere] * (4 + chips),
        out_specs=(anywhere,) * (1 + chips),
        scratch_shapes=[
            pltpu.VMEM((rows, width), jnp.bfloat16),
            pltpu.VMEM((rows, width), jnp.bfloat16),
            pltpu.VMEM((rows, LANES), jnp.bfloat16),
            pltpu.VMEM((groups, width), jnp.bfloat16),
            pltpu.VMEM((groups, hidden), jnp.bfloat16),
            pltpu.VMEM((width, hidden), jnp.bfloat16),
            pltpu.VMEM((width, hidden), jnp.bfloat16),
            pltpu.VMEM((hidden, width), jnp.bfloat16),
            pltpu.VMEM((rows, 2 * hidden), jnp.bfloat16),
            pltpu.VMEM((groups, width), jnp.float32),
            pltpu.VMEM((groups, hidden), jnp.float32),
            pltpu.VMEM((rows, hidden), jnp.float32),
            pltpu.VMEM((rows, hidden), jnp.float32),
            pltpu.VMEM((rows, groups), jnp.bfloat16),
            pltpu.VMEM((groups, rows), jnp.bfloat16),
            pltpu.VMEM((groups, rows), jnp.bfloat16),
            pltpu.VMEM((groups, hidden), jnp.bfloat16),
            pltpu.VMEM((groups, hidden), jnp.bfloat16),
            pltpu.SemaphoreType.DMA((2, 4)),
            pltpu.SemaphoreType.DMA((4 + 2 * chips,)),
            pltpu.SemaphoreType.DMA((2 * chips,)),
            pltpu.SemaphoreType.DMA((width // 1024,)),
        ],
        compiler_params=pltpu.CompilerParams(vmem_limit_bytes=EXPERT_VMEM_BYTES),
        cost_estimate=pl.CostEstimate(
            flops=10 * rows * width * hidden + 6 * rows * width * groups,
            bytes_accessed=6 * width * hidden + 6 * rows * width,
            transcendentals=rows * hidden,
        ),
        name="expert_pass",
    )(received, gate_matrix, up_matrix, down_weight, *held)


def along_x(rows, step):
    devices = lax.axis_size("dp")
    return lax.ppermute(rows, "dp", [(i, (i + 2 * step) % devices) for i in range(devices)])


def other_core(rows):
    return lax.ppermute(rows, "dp", [(i, i ^ 1) for i in range(lax.axis_size("dp"))])


def exchange(named, rows):
    return lax.cond(
        named,
        lambda r: lax.all_to_all(r, "expert", split_axis=0, concat_axis=0, tiled=True),
        jnp.zeros_like,
        rows,
    )


def local(
    tokens,
    cotangent,
    routed_expert_index,
    router_gate_weights,
    token_tenant_index,
    frozen_gate_weight,
    frozen_up_weight,
    frozen_down_weight,
    adapter_down_matrices,
    adapter_up_matrices,
):
    experts = lax.axis_size("expert")
    tenants = lax.axis_size("dp")
    tok_rows, width = tokens.shape
    routes = routed_expert_index.shape[1]
    hidden = frozen_gate_weight.shape[2]
    rank = adapter_down_matrices.shape[3]
    capacity = 5 * tok_rows * routes // (4 * experts)
    idx = routed_expert_index.T
    prob = router_gate_weights.T
    me = lax.axis_index("dp")
    chips = tenants // 2
    tenant = token_tenant_index.reshape(1, tok_rows)
    adapters = jnp.concatenate([adapter_down_matrices[0, 0], adapter_up_matrices[0, 0]], axis=-1)
    adapters = adapters.reshape(2 * rank, width + hidden)
    named = me < tenants
    sent = dispatch(me, idx, prob, tenant, tokens, cotangent, experts, capacity, chips)
    sent, others = lax.optimization_barrier((sent, other_core(adapters)))
    pair = jnp.concatenate([adapters, others], axis=0)
    held = [pair] + [along_x(pair, step) for step in range(1, chips)]
    received = exchange(named, sent)
    received, *held = lax.optimization_barrier((received, *held))
    route_grad, own, *parts = expert_pass(
        received,
        frozen_gate_weight[0],
        frozen_up_weight[0],
        frozen_down_weight[0],
        held,
        rank,
    )
    arrived = [along_x(part, -step) for step, part in enumerate(parts, 1)]
    returned = exchange(named, route_grad)
    returned, own, *arrived = lax.optimization_barrier((returned, own, *arrived))
    token_grads = combine(idx, returned, experts, capacity)
    total = sum(arrived, own)
    owned = total[: 2 * rank] + other_core(total[2 * rank :])
    down_owned = owned[:, :width].reshape(1, 1, 2, rank, width)
    up_owned = owned[:, width:].reshape(1, 1, 2, rank, hidden)
    return token_grads, down_owned, up_owned


def solution(mesh):
    in_specs = (
        P(("dp", "expert"), None),
        P(("dp", "expert"), None),
        P(("dp", "expert"), None),
        P(("dp", "expert"), None),
        P(("dp", "expert")),
        P("expert", None, None),
        P("expert", None, None),
        P("expert", None, None),
        P("dp", "expert", None, None, None),
        P("dp", "expert", None, None, None),
    )
    out_specs = (
        P(("dp", "expert"), None),
        P("dp", "expert", None, None, None),
        P("dp", "expert", None, None, None),
    )
    return jax.shard_map(local, mesh=mesh, in_specs=in_specs, out_specs=out_specs, check_vma=False)
```

```python
import functools

import jax
import jax.numpy as jnp
from jax import lax
from jax.experimental import pallas as pl
from jax.experimental.pallas import tpu as pltpu
from jax.sharding import PartitionSpec as P

adapter_scale = 0.5
LANES = 128
VMEM_BYTES = 60 * 1024 * 1024
EXPERT_VMEM_BYTES = 52 * 1024 * 1024


def contract_last(left_side, right_side):
    return lax.dot_general(
        left_side, right_side, (((1,), (1,)), ((), ())), preferred_element_type=jnp.float32
    )


def matmul(left_side, right_side):
    return jnp.dot(left_side, right_side, preferred_element_type=jnp.float32)


def route_slots(idx, experts, capacity):
    routes, tok_rows = idx.shape
    names = lax.broadcasted_iota(jnp.int32, (experts, tok_rows), 0)
    members = [(idx[k : k + 1, :] == names).astype(jnp.float32) for k in range(routes)]
    before = (
        lax.broadcasted_iota(jnp.int32, (tok_rows, tok_rows), 0)
        < lax.broadcasted_iota(jnp.int32, (tok_rows, tok_rows), 1)
    ).astype(jnp.bfloat16)
    running = matmul(sum(members).astype(jnp.bfloat16), before)
    return [
        idx[k : k + 1, :] * capacity
        + jnp.sum(running * member, axis=0, keepdims=True).astype(jnp.int32)
        for k, member in enumerate(members)
    ]


def dispatch_kernel(
    experts,
    capacity,
    chips,
    me_ref,
    idx_ref,
    prob_ref,
    tenant_ref,
    tok_ref,
    cot_ref,
    out_ref,
    select,
    weight,
    tenant_rows,
    feat_out,
    cot_out,
    sems,
    tenant_sem,
):
    step = pl.program_id(0)
    steps = pl.num_programs(0)
    block = tok_ref.shape[1]
    width = block * steps
    slot = lax.rem(step, 2)

    def copies(at, slot):
        column = pl.multiple_of(at * block, block)
        return (
            pltpu.make_async_copy(
                feat_out.at[slot], out_ref.at[:, pl.ds(column, block)], sems.at[0, slot]
            ),
            pltpu.make_async_copy(
                cot_out.at[slot], out_ref.at[:, pl.ds(width + column, block)], sems.at[1, slot]
            ),
        )

    tenant_copy = pltpu.make_async_copy(
        tenant_rows, out_ref.at[:, pl.ds(2 * width, LANES)], tenant_sem
    )

    @pl.when(step == 0)
    def _():
        rows = lax.broadcasted_iota(jnp.int32, select.shape, 0)
        masks = [rows == slots for slots in route_slots(idx_ref[...], experts, capacity)]
        filled = sum(m.astype(jnp.float32) for m in masks)
        weight[...] = sum(
            jnp.sum(jnp.where(m, prob_ref[k : k + 1, :], 0.0), axis=1, keepdims=True)
            for k, m in enumerate(masks)
        )
        me, owner = me_ref[0], tenant_ref[...]
        place = lax.rem(me // 2 + chips - lax.div(owner, 2), chips) * 2 + lax.rem(me + owner, 2)
        tenant = jnp.sum(filled * place.astype(jnp.float32), axis=1, keepdims=True)
        tenant_rows[...] = jnp.broadcast_to(tenant, tenant_rows.shape).astype(jnp.bfloat16)
        tenant_copy.start()
        select[...] = filled.astype(jnp.bfloat16)

    @pl.when(step >= 2)
    def _():
        for copy in copies(step - 2, slot):
            copy.wait()

    feat_out[slot] = matmul(select[...], tok_ref[...]).astype(jnp.bfloat16)
    cot_out[slot] = (matmul(select[...], cot_ref[...]) * weight[...]).astype(jnp.bfloat16)
    for copy in copies(step, slot):
        copy.start()

    @pl.when(step == steps - 1)
    def _():
        for copy in copies(step - 1, 1 - slot):
            copy.wait()
        for copy in copies(step, slot):
            copy.wait()
        tenant_copy.wait()


def dispatch(me, idx, prob, tenant, tokens, cotangent, experts, capacity, chips):
    tok_rows, width = tokens.shape
    rows = experts * capacity
    block = 2048
    return pl.pallas_call(
        functools.partial(dispatch_kernel, experts, capacity, chips),
        out_shape=jax.ShapeDtypeStruct((rows, 2 * width + LANES), jnp.bfloat16),
        grid=(width // block,),
        in_specs=[
            pl.BlockSpec(memory_space=pltpu.SMEM),
            pl.BlockSpec(idx.shape, lambda i: (0, 0)),
            pl.BlockSpec(prob.shape, lambda i: (0, 0)),
            pl.BlockSpec(tenant.shape, lambda i: (0, 0)),
            pl.BlockSpec((tok_rows, block), lambda i: (0, i)),
            pl.BlockSpec((tok_rows, block), lambda i: (0, i)),
        ],
        out_specs=pl.BlockSpec(memory_space=pl.ANY),
        scratch_shapes=[
            pltpu.VMEM((rows, tok_rows), jnp.bfloat16),
            pltpu.VMEM((rows, 1), jnp.float32),
            pltpu.VMEM((rows, LANES), jnp.bfloat16),
            pltpu.VMEM((2, rows, block), jnp.bfloat16),
            pltpu.VMEM((2, rows, block), jnp.bfloat16),
            pltpu.SemaphoreType.DMA((2, 2)),
            pltpu.SemaphoreType.DMA,
        ],
        compiler_params=pltpu.CompilerParams(vmem_limit_bytes=VMEM_BYTES),
        cost_estimate=pl.CostEstimate(
            flops=4 * rows * tok_rows * width,
            bytes_accessed=4 * tok_rows * width + 4 * rows * width,
            transcendentals=0,
        ),
        name="dispatch",
    )(me.reshape(1), idx, prob, tenant, tokens, cotangent)


def combine_kernel(experts, capacity, idx_ref, ret_ref, out_ref, select):
    @pl.when(pl.program_id(0) == 0)
    def _():
        slots = route_slots(idx_ref[...], experts, capacity)
        rows = lax.broadcasted_iota(jnp.int32, (8, slots[0].shape[1]), 0)
        table = sum(jnp.where(rows == k, s.astype(jnp.float32), 0.0) for k, s in enumerate(slots))
        table = table.T.astype(jnp.int32)
        lanes = lax.broadcasted_iota(jnp.int32, select.shape, 1)
        select[...] = sum(
            (lanes == table[:, k : k + 1]).astype(jnp.float32) for k in range(len(slots))
        ).astype(jnp.bfloat16)

    out_ref[...] = matmul(select[...], ret_ref[...]).astype(jnp.bfloat16)


def combine(idx, returned, experts, capacity):
    tok_rows, width = idx.shape[1], returned.shape[1]
    block = 2048
    rows = returned.shape[0]
    return pl.pallas_call(
        functools.partial(combine_kernel, experts, capacity),
        out_shape=jax.ShapeDtypeStruct((tok_rows, width), jnp.bfloat16),
        grid=(width // block,),
        in_specs=[
            pl.BlockSpec(idx.shape, lambda i: (0, 0)),
            pl.BlockSpec((rows, block), lambda i: (0, i)),
        ],
        out_specs=pl.BlockSpec((tok_rows, block), lambda i: (0, i)),
        scratch_shapes=[pltpu.VMEM((tok_rows, rows), jnp.bfloat16)],
        compiler_params=pltpu.CompilerParams(vmem_limit_bytes=VMEM_BYTES),
        cost_estimate=pl.CostEstimate(
            flops=2 * rows * tok_rows * width,
            bytes_accessed=2 * (rows + tok_rows) * width,
            transcendentals=0,
        ),
        name="combine",
    )(idx, returned)


def expert_kernel(
    rank,
    chips,
    got_ref,
    gate_ref,
    up_ref,
    down_ref,
    *refs,
):
    held_refs, route_out, part_outs = refs[:chips], refs[chips], refs[chips + 1 : 2 * chips + 1]
    expert_body(rank, got_ref, gate_ref, up_ref, down_ref, held_refs, route_out, part_outs, *refs[2 * chips + 1 :])


def expert_body(
    rank,
    got_ref,
    gate_ref,
    up_ref,
    down_ref,
    held_refs,
    route_out,
    part_outs,
    feat,
    cot,
    tenant,
    low_held,
    high_held,
    gate,
    up,
    down,
    grads,
    down_sum,
    up_sum,
    gate_pre,
    up_pre,
    low,
    low_t,
    back_t,
    high_gate,
    high_up,
    first_sems,
    sems,
    out_sems,
    route_sems,
):
    width = feat.shape[1]
    hidden = down.shape[0]
    groups, chip_rows = low_held.shape[0], held_refs[0].shape[0]
    block = 256
    step = 1024
    parts = hidden // block

    quarter = width // 4

    def first_copies(q):
        at = pl.ds(pl.multiple_of(q * quarter, quarter), quarter)
        return (
            pltpu.make_async_copy(got_ref.at[:, at], feat.at[:, at], first_sems.at[0, q]),
            pltpu.make_async_copy(gate_ref.at[at], gate.at[at], first_sems.at[1, q]),
        )

    later = [[], [], []]

    def plan(stage, source, target):
        number = sum(len(c) for c in later)
        later[stage].append(pltpu.make_async_copy(source, target, sems.at[number]))

    plan(0, got_ref.at[:, pl.ds(2 * width, LANES)], tenant)
    for c, held in enumerate(held_refs):
        rows = pl.ds(c * chip_rows, chip_rows)
        plan(0, held.at[:, pl.ds(0, width)], low_held.at[rows])
        plan(0, held.at[:, pl.ds(width, hidden)], high_held.at[rows])
    plan(1, up_ref, up)
    plan(2, got_ref.at[:, pl.ds(width, width)], cot)
    plan(2, down_ref, down)

    def begin(copies):
        for copy in copies:
            copy.start()

    def arrive(copies):
        for copy in copies:
            copy.wait()

    begin(first_copies(0))
    begin(first_copies(1))
    gate_pre[...] = jnp.zeros_like(gate_pre)

    def gate_step(q, carry):
        arrive(first_copies(q))
        pl.when(q < 2)(lambda: begin(first_copies(q + 2)))
        pl.when(q == 2)(lambda: begin(later[0]))
        pl.when(q == 3)(lambda: begin(later[1]))
        at = pl.ds(pl.multiple_of(q * quarter, quarter), quarter)
        for h in range(parts):
            to = slice(h * block, (h + 1) * block)
            gate_pre[:, to] += matmul(feat[:, at], gate[at, to])
        return carry

    lax.fori_loop(0, 4, gate_step, 0)
    arrive(later[0])
    begin(later[2])
    owner = lax.broadcasted_iota(jnp.int32, (1, groups), 1) // (2 * rank)
    selector = (tenant[:, 0:1].astype(jnp.int32) == owner).astype(jnp.float32)
    low[...] = (contract_last(feat[...], low_held[...]) * selector).astype(jnp.bfloat16)
    is_gate = lax.broadcasted_iota(jnp.int32, (groups, 1), 0) // rank % 2 == 0
    high = high_held[...].astype(jnp.float32)
    high_gate[...] = jnp.where(is_gate, high, 0.0).astype(jnp.bfloat16)
    high_up[...] = jnp.where(is_gate, 0.0, high).astype(jnp.bfloat16)
    arrive(later[1])

    def up_step(h, carry):
        at = pl.ds(pl.multiple_of(h * block, block), block)
        up_pre[:, at] = matmul(feat[...], up[:, at]) + adapter_scale * matmul(
            low[...], high_up[:, at]
        )
        return carry

    lax.fori_loop(0, parts, up_step, 0)
    arrive(later[2])

    def back_step(h, carry):
        at = pl.ds(pl.multiple_of(h * block, block), block)
        after = pl.ds(pl.multiple_of(hidden + h * block, block), block)
        back = contract_last(cot[...], down[at])
        pre = gate_pre[:, at] + adapter_scale * matmul(low[...], high_gate[:, at])
        sig = jax.nn.sigmoid(pre)
        grads[:, at] = (back * up_pre[:, at] * (sig + pre * sig * (1.0 - sig))).astype(jnp.bfloat16)
        grads[:, after] = (back * pre * sig).astype(jnp.bfloat16)
        return carry

    lax.fori_loop(0, parts, back_step, 0)
    low_back = contract_last(grads[:, :hidden], high_gate[...]) + contract_last(
        grads[:, hidden:], high_up[...]
    )
    low_back = (low_back * selector).astype(jnp.bfloat16)
    back_t[...] = low_back.astype(jnp.float32).T.astype(jnp.bfloat16)
    low_t[...] = low[...].astype(jnp.float32).T.astype(jnp.bfloat16)
    low[...] = low_back

    for h in range(parts):
        at = pl.ds(h * block, block)
        after = pl.ds(hidden + h * block, block)
        up_sum[:, at] = adapter_scale * jnp.where(
            is_gate, matmul(low_t[...], grads[:, at]), matmul(low_t[...], grads[:, after])
        )
    for i in range(width // step):
        at = pl.ds(i * step, step)
        down_sum[:, at] = adapter_scale * matmul(back_t[...], feat[:, at])
    leaving = []
    for c, part_out in enumerate(part_outs):
        rows = pl.ds(c * chip_rows, chip_rows)
        for source, at in ((up_sum, pl.ds(width, hidden)), (down_sum, pl.ds(0, width))):
            leaving.append(
                pltpu.make_async_copy(source.at[rows], part_out.at[:, at], out_sems.at[len(leaving)])
            )
    begin(leaving)

    def route_copy(i):
        at = pl.ds(i * step, step)
        return pltpu.make_async_copy(cot.at[:, at], route_out.at[:, at], route_sems.at[i])

    for i in range(width // step):
        at = pl.ds(i * step, step)
        cot[:, at] = (
            contract_last(grads[:, :hidden], gate[at])
            + contract_last(grads[:, hidden:], up[at])
            + adapter_scale * matmul(low[...], low_held[:, at])
        ).astype(jnp.bfloat16)
        route_copy(i).start()
    arrive(leaving)
    for i in range(width // step):
        route_copy(i).wait()


def expert_pass(received, gate_matrix, up_matrix, down_weight, held, rank):
    rows = received.shape[0]
    width, hidden = gate_matrix.shape
    chips, chip_rows = len(held), held[0].shape[0]
    groups = chips * chip_rows
    anywhere = pl.BlockSpec(memory_space=pl.ANY)
    return pl.pallas_call(
        functools.partial(expert_kernel, rank, chips),
        out_shape=(
            jax.ShapeDtypeStruct((rows, width), jnp.bfloat16),
            *[jax.ShapeDtypeStruct((chip_rows, width + hidden), jnp.float32)] * chips,
        ),
        in_specs=[anywhere] * (4 + chips),
        out_specs=(anywhere,) * (1 + chips),
        scratch_shapes=[
            pltpu.VMEM((rows, width), jnp.bfloat16),
            pltpu.VMEM((rows, width), jnp.bfloat16),
            pltpu.VMEM((rows, LANES), jnp.bfloat16),
            pltpu.VMEM((groups, width), jnp.bfloat16),
            pltpu.VMEM((groups, hidden), jnp.bfloat16),
            pltpu.VMEM((width, hidden), jnp.bfloat16),
            pltpu.VMEM((width, hidden), jnp.bfloat16),
            pltpu.VMEM((hidden, width), jnp.bfloat16),
            pltpu.VMEM((rows, 2 * hidden), jnp.bfloat16),
            pltpu.VMEM((groups, width), jnp.float32),
            pltpu.VMEM((groups, hidden), jnp.float32),
            pltpu.VMEM((rows, hidden), jnp.float32),
            pltpu.VMEM((rows, hidden), jnp.float32),
            pltpu.VMEM((rows, groups), jnp.bfloat16),
            pltpu.VMEM((groups, rows), jnp.bfloat16),
            pltpu.VMEM((groups, rows), jnp.bfloat16),
            pltpu.VMEM((groups, hidden), jnp.bfloat16),
            pltpu.VMEM((groups, hidden), jnp.bfloat16),
            pltpu.SemaphoreType.DMA((2, 4)),
            pltpu.SemaphoreType.DMA((4 + 2 * chips,)),
            pltpu.SemaphoreType.DMA((2 * chips,)),
            pltpu.SemaphoreType.DMA((width // 1024,)),
        ],
        compiler_params=pltpu.CompilerParams(vmem_limit_bytes=EXPERT_VMEM_BYTES),
        cost_estimate=pl.CostEstimate(
            flops=10 * rows * width * hidden + 6 * rows * width * groups,
            bytes_accessed=6 * width * hidden + 6 * rows * width,
            transcendentals=rows * hidden,
        ),
        name="expert_pass",
    )(received, gate_matrix, up_matrix, down_weight, *held)


def along_x(rows, step):
    devices = lax.axis_size("dp")
    return lax.ppermute(rows, "dp", [(i, (i + 2 * step) % devices) for i in range(devices)])


def other_core(rows):
    return lax.ppermute(rows, "dp", [(i, i ^ 1) for i in range(lax.axis_size("dp"))])


def exchange(named, rows):
    return lax.cond(
        named,
        lambda r: lax.all_to_all(r, "expert", split_axis=0, concat_axis=0, tiled=True),
        jnp.zeros_like,
        rows,
    )


def local(
    tokens,
    cotangent,
    routed_expert_index,
    router_gate_weights,
    token_tenant_index,
    frozen_gate_weight,
    frozen_up_weight,
    frozen_down_weight,
    adapter_down_matrices,
    adapter_up_matrices,
):
    experts = lax.axis_size("expert")
    tenants = lax.axis_size("dp")
    tok_rows, width = tokens.shape
    routes = routed_expert_index.shape[1]
    hidden = frozen_gate_weight.shape[2]
    rank = adapter_down_matrices.shape[3]
    capacity = 5 * tok_rows * routes // (4 * experts)
    idx = routed_expert_index.T
    prob = router_gate_weights.T
    me = lax.axis_index("dp")
    chips = tenants // 2
    tenant = token_tenant_index.reshape(1, tok_rows)
    adapters = jnp.concatenate([adapter_down_matrices[0, 0], adapter_up_matrices[0, 0]], axis=-1)
    adapters = adapters.reshape(2 * rank, width + hidden)
    named = me < tenants
    sent = dispatch(me, idx, prob, tenant, tokens, cotangent, experts, capacity, chips)
    sent, others = lax.optimization_barrier((sent, other_core(adapters)))
    pair = jnp.concatenate([adapters, others], axis=0)
    held = [pair] + [along_x(pair, step) for step in range(1, chips)]
    received = exchange(named, sent)
    received, *held = lax.optimization_barrier((received, *held))
    route_grad, own, *parts = expert_pass(
        received,
        frozen_gate_weight[0],
        frozen_up_weight[0],
        frozen_down_weight[0],
        held,
        rank,
    )
    arrived = [along_x(part, -step) for step, part in enumerate(parts, 1)]
    returned = exchange(named, route_grad)
    returned, own, *arrived = lax.optimization_barrier((returned, own, *arrived))
    token_grads = combine(idx, returned, experts, capacity)
    theirs = sum((part[2 * rank :] for part in arrived), own[2 * rank :])
    mine = sum((part[: 2 * rank] for part in arrived), own[: 2 * rank])
    owned = mine + other_core(theirs)
    down_owned = owned[:, :width].reshape(1, 1, 2, rank, width)
    up_owned = owned[:, width:].reshape(1, 1, 2, rank, hidden)
    return token_grads, down_owned, up_owned


def solution(mesh):
    in_specs = (
        P(("dp", "expert"), None),
        P(("dp", "expert"), None),
        P(("dp", "expert"), None),
        P(("dp", "expert"), None),
        P(("dp", "expert")),
        P("expert", None, None),
        P("expert", None, None),
        P("expert", None, None),
        P("dp", "expert", None, None, None),
        P("dp", "expert", None, None, None),
    )
    out_specs = (
        P(("dp", "expert"), None),
        P("dp", "expert", None, None, None),
        P("dp", "expert", None, None, None),
    )
    return jax.shard_map(local, mesh=mesh, in_specs=in_specs, out_specs=out_specs, check_vma=False)
```
